32 devices in a mesh: batch: 8 (over y, x, core), row: 4 (over z).
Axes of the slice: x: 2, y: 2, z: 4, core: 2. Of those that a mesh axis runs over, the one named last changes fastest.
Arguments:
- images: bfloat16 [2, 64, 128, 1536], P(None, 'batch', 'row'), may hold values from -6 to 6
- bucket: int32 [2, 64], P(None, 'batch'), may hold values 0 or 1
- cotangent: bfloat16 [2, 64, 128, 1536], P(None, 'batch', 'row'), may hold values from -6 to 6
- narrow_kernel: bfloat16 [768, 1536], P(('batch', 'row')), may hold values from -0.15625 to 0.15625
- narrow_gain: bfloat16 [768], P(('batch', 'row')), may hold values from 0.25 to 1.75
- narrow_bias: bfloat16 [768], P(('batch', 'row')), may hold values from -3 to 3
- first_kernel: bfloat16 [768, 1152], P(('batch', 'row')), may hold values from -0.1875 to 0.1875
- first_gain: bfloat16 [768], P(('batch', 'row')), may hold values from 0.25 to 1.75
- first_bias: bfloat16 [768], P(('batch', 'row')), may hold values from -3 to 3
- second_kernel: bfloat16 [768, 1152], P(('batch', 'row')), may hold values from -0.1875 to 0.1875
- second_gain: bfloat16 [768], P(('batch', 'row')), may hold values from 0.25 to 1.75
- second_bias: bfloat16 [768], P(('batch', 'row')), may hold values from -3 to 3
- widen_kernel: bfloat16 [1536, 768], P(('batch', 'row')), may hold values from -0.21875 to 0.21875
- widen_gain: bfloat16 [1536], P(('batch', 'row')), may hold values from 0.25 to 1.75
- widen_bias: bfloat16 [1536], P(('batch', 'row')), may hold values from -3 to 3
- squeeze_kernel: bfloat16 [768, 1536], P(('batch', 'row')), may hold values from -0.625 to 0.625
- squeeze_bias: bfloat16 [768], P(('batch', 'row')), may hold values from -3 to 3
- excite_kernel: bfloat16 [1536, 768], P(('batch', 'row')), may hold values from -0.4375 to 0.4375
- excite_bias: bfloat16 [1536], P(('batch', 'row')), may hold values from -3 to 3
- skip_gain: bfloat16 [1], replicated, may hold values from 3 to 6
Outputs:
- output: bfloat16 [2, 64, 128, 1536], P(None, 'batch', 'row')
- input_grad: bfloat16 [2, 64, 128, 1536], P(None, 'batch', 'row')
- narrow_kernel_grad: float32 [768, 1536], P(('batch', 'row'))
- narrow_gain_grad: float32 [768], P(('batch', 'row'))
- narrow_bias_grad: float32 [768], P(('batch', 'row'))
- first_kernel_grad: float32 [768, 1152], P(('batch', 'row'))
- first_gain_grad: float32 [768], P(('batch', 'row'))
- first_bias_grad: float32 [768], P(('batch', 'row'))
- second_kernel_grad: float32 [768, 1152], P(('batch', 'row'))
- second_gain_grad: float32 [768], P(('batch', 'row'))
- second_bias_grad: float32 [768], P(('batch', 'row'))
- widen_kernel_grad: float32 [1536, 768], P(('batch', 'row'))
- widen_gain_grad: float32 [1536], P(('batch', 'row'))
- widen_bias_grad: float32 [1536], P(('batch', 'row'))
- squeeze_kernel_grad: float32 [768, 1536], P(('batch', 'row'))
- squeeze_bias_grad: float32 [768], P(('batch', 'row'))
- excite_kernel_grad: float32 [1536, 768], P(('batch', 'row'))
- excite_bias_grad: float32 [1536], P(('batch', 'row'))
- skip_gain_grad: float32 [1], replicated
The draws below stay inside these ranges and needn't reach their ends.
All inputs are finite; a program needn't handle non-finite values. No bound on the sum of `bucket` on one device may be relied on, other than what follows from the above.
Results may differ from the reference program's by a relative error of at most 0.04.
Values may be sent and summed in bfloat16 or wider, within the bound.
A program may use at most 192 MiB of HBM per device.

```python
import math
import jax
import jax.numpy as jnp
from jax import lax

D = 1536
MID = 768
GW = 128
PIX = 128
MICRO = 2
IMG = 64


def touch_ends(entries, own_key, smallest, high):
    dims = entries.shape
    index_at = [jax.random.randint(jax.random.fold_in(own_key, axis), (), 0, dims[axis]) for axis in range(len(dims))]
    entries = entries.at[tuple(index_at)].set(smallest)
    longest = dims.index(max(dims))
    index_at[longest] = (index_at[longest] + 1) % dims[longest]
    return entries.at[tuple(index_at)].set(high)


def raised(drawn, stream_key, source, target, shards_of, factor):
    owner, partner = [(jnp.arange(drawn.shape[dim]) // (drawn.shape[dim] // shards_of)).reshape([-1 if axis == dim else 1 for axis in range(drawn.ndim)]) for dim in (source, target)]
    chosen = jax.random.permutation(stream_key, shards_of)[partner]
    strong = (owner == chosen) | (owner == (partner + shards_of // 2) % shards_of)
    return jnp.where(strong, factor * drawn, drawn)


def shard_levels(own_key, shape, shards, least, top_value):
    factor_of, own = 1.0, jax.random.fold_in(own_key, 6)
    for position, blocks in shards:
        heights = jnp.exp(jax.random.uniform(jax.random.fold_in(own, position), (blocks,), jnp.float32, least / len(shards), top_value / len(shards)))
        factor_of = factor_of * jnp.repeat(heights, shape[position] // blocks).reshape([-1 if axis == position else 1 for axis in range(len(shape))])
    return factor_of


def scatter_about(own_key, dims, scale, bound, cuts=(), dtype=jnp.bfloat16):
    values = scale * jax.random.normal(own_key, dims, jnp.float32)
    if cuts:
        values = values * shard_levels(own_key, dims, cuts, -0.22, 0.18)
    return jnp.clip(values, -bound, bound).astype(dtype)


def bell_draw_with(rng, shape, deviation, bound, shards, heavy, kind=jnp.bfloat16):
    values = deviation * jax.random.normal(rng, shape, jnp.float32)
    if shards:
        values = values * shard_levels(rng, shape, shards, -0.22, 0.18)
    return jnp.clip(raised(values, jax.random.fold_in(rng, 3), *heavy), -bound, bound).astype(kind)


def setup_inputs(seed: int = 0) -> dict:
    splits = jax.random.split(jax.random.key(seed), 21)
    images = scatter_about(splits[0], (MICRO, IMG, PIX, D), 1.0, 6.0, ((1, 8), (2, 4)))
    bucket = touch_ends((jax.random.randint(splits[1], (MICRO, IMG), 0, 928) < 384).astype(jnp.int32), jax.random.fold_in(splits[1], 1), 0, 1)
    cotangent = bell_draw_with(splits[2], (MICRO, IMG, PIX, D), 1.0, 6.0, ((1, 8), (2, 4)), (1, 3, 8, 2.0))
    narrow_kernel = scatter_about(splits[3], (MID, D), D ** -0.5, 0.15625, ((0, 32),))
    narrow_gain = jnp.clip(1.0 + 0.15 * jax.random.normal(splits[4], (MID,), jnp.float32), 0.25, 1.75).astype(jnp.bfloat16)
    narrow_bias = scatter_about(splits[5], (MID,), 0.3, 3.0, ((0, 32),))
    first_kernel = scatter_about(splits[6], (MID, 9 * GW), (9 * GW) ** -0.5, 0.1875, ((0, 32),))
    first_gain = jnp.clip(1.0 + 0.15 * jax.random.normal(splits[7], (MID,), jnp.float32), 0.25, 1.75).astype(jnp.bfloat16)
    first_bias = scatter_about(splits[8], (MID,), 0.3, 3.0, ((0, 32),))
    second_kernel = scatter_about(splits[9], (MID, 9 * GW), (9 * GW) ** -0.5, 0.1875, ((0, 32),))
    second_gain = jnp.clip(1.0 + 0.15 * jax.random.normal(splits[10], (MID,), jnp.float32), 0.25, 1.75).astype(jnp.bfloat16)
    second_bias = scatter_about(splits[11], (MID,), 0.3, 3.0, ((0, 32),))
    widen_kernel = scatter_about(splits[12], (D, MID), MID ** -0.5, 0.21875, ((0, 32),))
    widen_gain = jnp.clip(1.0 + 0.15 * jax.random.normal(splits[13], (D,), jnp.float32), 0.25, 1.75).astype(jnp.bfloat16)
    widen_bias = scatter_about(splits[14], (D,), 0.3, 3.0, ((0, 32),))
    squeeze_kernel = scatter_about(splits[15], (MID, D), (D // 16) ** -0.5, 0.625, ((0, 32),))
    squeeze_bias = scatter_about(splits[16], (MID,), 0.3, 3.0, ((0, 32),))
    excite_kernel = scatter_about(splits[17], (D, MID), (MID // 4) ** -0.5, 0.4375, ((0, 32),))
    excite_bias = scatter_about(splits[18], (D,), 0.3, 3.0, ((0, 32),))
    skip_gain = jnp.clip(jax.random.uniform(splits[19], (1,), jnp.float32, 3.0, 6.0), 3.0, 6.0).astype(jnp.bfloat16)
    return dict(images=images, bucket=bucket, cotangent=cotangent, narrow_kernel=narrow_kernel, narrow_gain=narrow_gain, narrow_bias=narrow_bias, first_kernel=first_kernel, first_gain=first_gain, first_bias=first_bias, second_kernel=second_kernel, second_gain=second_gain, second_bias=second_bias, widen_kernel=widen_kernel, widen_gain=widen_gain, widen_bias=widen_bias, squeeze_kernel=squeeze_kernel, squeeze_bias=squeeze_bias, excite_kernel=excite_kernel, excite_bias=excite_bias, skip_gain=skip_gain)


@jax.custom_vjp
def low(v):
    return lax.optimization_barrier(v.astype(jnp.bfloat16)).astype(jnp.float32)

@jax.custom_vjp
def low_back(v):
    return v

def low_keep(v):
    return (low(v), None)

def low_pass(kept, grad):
    return (grad,)

def back_keep(v):
    return (v, None)

def back_low(kept, grad):
    return (low(grad),)
low.defvjp(low_keep, low_pass)
low_back.defvjp(back_keep, back_low)
gamma_act = 1.7015
alpha_res = 0.2
beta_in = 0.9622504486493763
eps_std = 0.0001
highest = lax.Precision.HIGHEST

def scaled_gelu(value):
    return gamma_act * jax.nn.gelu(value)

def standard(kernel, gain):
    fan = kernel.shape[1]
    center = lax.optimization_barrier(jnp.mean(kernel, axis=1, keepdims=True))
    spread_sq = lax.optimization_barrier(jnp.mean(jnp.square(kernel - center), axis=1, keepdims=True))
    return gain[:, None] * (kernel - center) * lax.rsqrt(fan * spread_sq + eps_std)

def shifted_maps(field, wide):
    padded = jnp.pad(field, ((0, 0), (17, 17), (0, 0)))
    places = jnp.arange(PIX)
    pieces = []
    for step_row in (-1, 0, 1):
        for step_col in (-1, 0, 1):
            start_wide = 17 + step_row * 16 + step_col
            start_tall = 17 + step_row * 8 + step_col
            wide_part = padded[:, start_wide:start_wide + PIX]
            tall_part = padded[:, start_tall:start_tall + PIX]
            wide_ok = (places % 16 + step_col >= 0) & (places % 16 + step_col < 16)
            tall_ok = (places % 8 + step_col >= 0) & (places % 8 + step_col < 8)
            keep = jnp.where(wide[:, None], wide_ok[None, :], tall_ok[None, :])
            chosen = jnp.where(wide[:, None, None], wide_part, tall_part)
            pieces.append(jnp.where(keep[:, :, None], chosen, jnp.zeros_like(chosen)))
    return pieces

def grouped(field, kernel, wide):
    blocks = field.shape[0]
    groups = kernel.shape[0] // GW
    shaped = kernel.reshape(groups, GW, 9, GW)
    total = jnp.zeros((blocks, PIX, groups, GW), jnp.float32)
    for place, piece in enumerate(shifted_maps(field, wide)):
        total = total + jnp.einsum('bpgi,goi->bpgo', piece.reshape(blocks, PIX, groups, GW), shaped[:, :, place, :], precision=highest)
    return total.reshape(blocks, PIX, groups * GW)

def forward(params, inputs, wide):
    narrow_kernel, narrow_gain, narrow_bias, first_kernel, first_gain, first_bias, second_kernel, second_gain, second_bias, widen_kernel, widen_gain, widen_bias, squeeze_kernel, squeeze_bias, excite_kernel, excite_bias, skip_gain = params
    narrow_std = low(standard(narrow_kernel, narrow_gain))
    first_std = low(standard(first_kernel, first_gain))
    second_std = low(standard(second_kernel, second_gain))
    widen_std = low(standard(widen_kernel, widen_gain))
    act_zero = low(scaled_gelu(inputs) * beta_in)
    pre_zero = low_back(jnp.einsum('bpd,md->bpm', act_zero, narrow_std, precision=highest)) + narrow_bias
    act_one = low(scaled_gelu(pre_zero))
    pre_one = low_back(grouped(act_one, first_std, wide)) + first_bias
    act_two = low(scaled_gelu(pre_one))
    pre_two = low_back(grouped(act_two, second_std, wide)) + second_bias
    act_three = low(scaled_gelu(pre_two))
    branch = low_back(jnp.einsum('bpm,dm->bpd', act_three, widen_std, precision=highest)) + widen_bias
    pooled = low(lax.optimization_barrier(jnp.mean(branch, axis=1)))
    squeezed = low_back(jnp.einsum('bd,md->bm', pooled, squeeze_kernel, precision=highest)) + squeeze_bias
    hidden = low(jax.nn.gelu(squeezed))
    excited = low_back(jnp.einsum('bm,dm->bd', hidden, excite_kernel, precision=highest)) + excite_bias
    gate = 2.0 * jax.nn.sigmoid(excited)
    return inputs + alpha_res * skip_gain[0] * (gate[:, None, :] * branch)

def reference(images, bucket, cotangent, narrow_kernel, narrow_gain, narrow_bias, first_kernel, first_gain, first_bias, second_kernel, second_gain, second_bias, widen_kernel, widen_gain, widen_bias, squeeze_kernel, squeeze_bias, excite_kernel, excite_bias, skip_gain):
    params = tuple((array.astype(jnp.float32) for array in (narrow_kernel, narrow_gain, narrow_bias, first_kernel, first_gain, first_bias, second_kernel, second_gain, second_bias, widen_kernel, widen_gain, widen_bias, squeeze_kernel, squeeze_bias, excite_kernel, excite_bias, skip_gain)))
    block = math.gcd(IMG, 32)
    steps_total = MICRO * IMG // block
    image_blocks = images.reshape(steps_total, block, PIX, D)
    bucket_blocks = bucket.reshape(steps_total, block)
    cotan_blocks = cotangent.reshape(steps_total, block, PIX, D)

    def step(totals, item):
        inputs, kinds, cotan = item
        wide = kinds == 0
        result, pull = jax.vjp(lambda weights, values: forward(weights, values, wide), params, inputs.astype(jnp.float32))
        weight_grads, input_grads = pull(cotan.astype(jnp.float32))
        totals = tuple((left + right for left, right in zip(totals, weight_grads)))
        return (totals, (result.astype(jnp.bfloat16), input_grads.astype(jnp.bfloat16)))
    start = tuple((jnp.zeros_like(array) for array in params))
    totals, (results, input_grads) = lax.scan(step, start, (image_blocks, bucket_blocks, cotan_blocks))
    output = results.reshape(MICRO, IMG, PIX, D)
    input_grad = input_grads.reshape(MICRO, IMG, PIX, D)
    return (output, input_grad, totals[0], totals[1], totals[2], totals[3], totals[4], totals[5], totals[6], totals[7], totals[8], totals[9], totals[10], totals[11], totals[12], totals[13], totals[14], totals[15], totals[16])
```

```python
import functools
import jax
import jax.numpy as jnp
from jax import lax
from jax.experimental import pallas as pl
from jax.experimental.pallas import tpu as pltpu
from jax.sharding import PartitionSpec as P

MESH = pl.DeviceIdType.MESH
BF = jnp.bfloat16
F32 = jnp.float32
GATHER_COPIES = 11
SCATTER_COPIES = 11


def place():
    return lax.axis_index("batch"), lax.axis_index("row")


def flip(value, bit):
    return lax.bitwise_xor(value, jnp.int32(bit))


def greet():
    b, z = place()
    barrier = pltpu.get_barrier_semaphore()
    for bit in (1, 2, 4):
        pl.semaphore_signal(barrier, inc=1, device_id=(flip(b, bit), z), device_id_type=MESH)
    for bit in (1, 2, 3):
        pl.semaphore_signal(barrier, inc=1, device_id=(b, flip(z, bit)), device_id_type=MESH)
    pl.semaphore_wait(barrier, 6)


class Gather:
    def __init__(self, slots, whole, send, recv):
        self.slots, self.whole, self.send, self.recv = slots, whole, send, recv
        self.rows = slots.shape[1]
        self.block = 4 * self.rows
        self.half = self.block // 2
        self.copies = {}

    def copy(self, key, src, dst, device):
        made = pltpu.make_async_remote_copy(
            src_ref=src, dst_ref=dst, send_sem=self.send.at[key], recv_sem=self.recv.at[key],
            device_id=device, device_id_type=MESH)
        made.start()
        self.copies[key] = made

    def at(self, index, start=0, size=None):
        size = self.block if size is None else size
        return self.whole.at[pl.ds(pl.multiple_of(index * self.block + start, 16), size)]

    def along_row(self):
        b, z = place()
        for j in (1, 2, 3):
            self.copy(j - 1, self.slots.at[z], self.slots.at[z], (b, flip(z, j)))

    def own_block(self):
        b, z = place()
        for j in (1, 2, 3):
            self.copies[j - 1].wait_recv()
        base = pl.multiple_of(b * self.block, 16)
        if self.rows % 16 == 0:
            for r in range(4):
                self.whole[pl.ds(base + r * self.rows, self.rows)] = self.slots[r]
        else:
            for r in (0, 2):
                pair = jnp.concatenate([self.slots[r].astype(F32), self.slots[r + 1].astype(F32)], axis=0)
                self.whole[pl.ds(base + r * self.rows, 2 * self.rows)] = pair.astype(self.whole.dtype)
        own = self.at(b)
        self.copy(3, own, own, (flip(b, 2), z))
        self.copy(4, own, own, (flip(b, 4), z))
        self.copy(5, own, own, (flip(b, 1), z))

    def onward(self):
        b, z = place()
        self.copies[3].wait_recv()
        low = self.at(flip(b, 2), 0, self.half)
        self.copy(6, low, low, (flip(b, 4), z))
        near = self.at(flip(b, 2))
        self.copy(8, near, near, (flip(b, 1), z))
        self.copies[4].wait_recv()
        high = self.at(flip(b, 4), self.half, self.half)
        self.copy(7, high, high, (flip(b, 2), z))
        near = self.at(flip(b, 4))
        self.copy(9, near, near, (flip(b, 1), z))

    def corner(self):
        b, z = place()
        self.copies[6].wait_recv()
        self.copies[7].wait_recv()
        far = self.at(flip(b, 6))
        self.copy(10, far, far, (flip(b, 1), z))

    def ready(self):
        for key in (5, 8, 9, 10):
            self.copies[key].wait_recv()

    def close(self):
        for key in range(GATHER_COPIES):
            self.copies[key].wait_send()


class Scatter:
    def __init__(self, whole, mate, diagonal, sides, pieces, landed, send, recv):
        self.whole, self.mate, self.diagonal, self.sides = whole, mate, diagonal, sides
        self.pieces, self.landed, self.send, self.recv = pieces, landed, send, recv
        self.rows = pieces.shape[1]
        self.block = 4 * self.rows
        self.half = self.block // 2
        self.copies = {}

    copy = Gather.copy
    at = Gather.at

    def to_mate(self):
        b, z = place()
        for k, q in enumerate((6, 2, 4, 0)):
            self.copy(k, self.at(flip(b, 1 ^ q)), self.mate.at[k], (flip(b, 1), z))

    def add(self, index, start, size, ref):
        where = pl.ds(pl.multiple_of(index * self.block + start, 16), size)
        total = self.whole[where].astype(F32) + ref[...].astype(F32)
        self.whole[where] = total.astype(self.whole.dtype)

    def diagonals(self):
        b, z = place()
        self.copies[0].wait_recv()
        self.add(flip(b, 6), 0, self.block, self.mate.at[0])
        self.copy(4, self.at(flip(b, 6), 0, self.half), self.diagonal.at[0], (flip(b, 4), z))
        self.copy(5, self.at(flip(b, 6), self.half, self.half), self.diagonal.at[1], (flip(b, 2), z))
        self.copies[1].wait_recv()
        self.add(flip(b, 2), 0, self.block, self.mate.at[1])
        self.copies[2].wait_recv()
        self.add(flip(b, 4), 0, self.block, self.mate.at[2])
        self.copies[3].wait_recv()
        self.add(b, 0, self.block, self.mate.at[3])

    def to_sides(self):
        b, z = place()
        self.copies[4].wait_recv()
        self.add(flip(b, 2), 0, self.half, self.diagonal.at[0])
        self.copy(6, self.at(flip(b, 2)), self.sides.at[0], (flip(b, 2), z))
        self.copies[5].wait_recv()
        self.add(flip(b, 4), self.half, self.half, self.diagonal.at[1])
        self.copy(7, self.at(flip(b, 4)), self.sides.at[1], (flip(b, 4), z))

    def along_row(self):
        b, z = place()
        self.copies[6].wait_recv()
        self.copies[7].wait_recv()
        for r in range(4):
            start = r * self.rows
            if self.rows % 16 == 0:
                part = self.whole[pl.ds(pl.multiple_of(b * self.block + start, 16), self.rows)].astype(F32)
                for side in (0, 1):
                    part += self.sides[side, start:start + self.rows].astype(F32)
                self.pieces[r] = part.astype(self.pieces.dtype)
            elif r % 2 == 0:
                size = 2 * self.rows
                part = self.whole[pl.ds(pl.multiple_of(b * self.block + start, 16), size)].astype(F32)
                for side in (0, 1):
                    part += self.sides[side, start:start + size].astype(F32)
                self.pieces[r] = part[:self.rows].astype(self.pieces.dtype)
                self.pieces[r + 1] = part[self.rows:].astype(self.pieces.dtype)
        for j in (1, 2, 3):
            self.copy(7 + j, self.pieces.at[flip(z, j)], self.landed.at[j - 1], (b, flip(z, j)))

    def total(self):
        b, z = place()
        result = self.pieces[z].astype(F32)
        for j in (1, 2, 3):
            self.copies[7 + j].wait_recv()
            result += self.landed[j - 1].astype(F32)
        return result

    def close(self):
        for key in range(SCATTER_COPIES):
            self.copies[key].wait_send()


def gather_kernel(count, *refs):
    shards, wholes, slots = refs[:count], refs[count:2 * count], refs[2 * count:3 * count]
    send, recv = refs[3 * count:]
    b, z = place()
    greet()
    jobs = []
    for i in range(count):
        slots[i][z] = shards[i][...]
        job = Gather(slots[i], wholes[i], send.at[i], recv.at[i])
        job.along_row()
        jobs.append(job)
    for step in range(count + 2):
        if step < count:
            jobs[step].own_block()
        if 0 <= step - 1 < count:
            jobs[step - 1].onward()
        if 0 <= step - 2 < count:
            jobs[step - 2].corner()
    for job in jobs:
        job.ready()
    for job in jobs:
        job.close()


def gather_all(shards, devices, collective):
    count = len(shards)
    vmem = pl.BlockSpec(memory_space=pltpu.VMEM)
    return pl.pallas_call(
        functools.partial(gather_kernel, count),
        out_shape=[jax.ShapeDtypeStruct((devices * s.shape[0], s.shape[1]), s.dtype) for s in shards],
        in_specs=[vmem] * count, out_specs=[vmem] * count,
        scratch_shapes=[pltpu.VMEM((4,) + s.shape, s.dtype) for s in shards]
        + [pltpu.SemaphoreType.DMA((count, GATHER_COPIES))] * 2,
        compiler_params=pltpu.CompilerParams(
            collective_id=collective, has_side_effects=True, vmem_limit_bytes=60 << 20),
    )(*shards)


def scatter_kernel(count, *refs):
    wholes, totals, scratch = refs[:count], refs[count:2 * count], refs[2 * count:]
    work, mates, diagonals, sides, pieces, landed = [scratch[i * count:(i + 1) * count] for i in range(6)]
    send, recv = scratch[6 * count:]
    greet()
    jobs = []
    for i in range(count):
        work[i][...] = wholes[i][...]
        job = Scatter(work[i], mates[i], diagonals[i], sides[i], pieces[i], landed[i], send.at[i], recv.at[i])
        job.to_mate()
        jobs.append(job)
    for step in range(count + 3):
        if step < count:
            jobs[step].diagonals()
        if 0 <= step - 1 < count:
            jobs[step - 1].to_sides()
        if 0 <= step - 2 < count:
            jobs[step - 2].along_row()
        if 0 <= step - 3 < count:
            totals[step - 3][...] = jobs[step - 3].total()
    for job in jobs:
        job.close()


def scatter_all(wholes, devices, collective):
    count = len(wholes)
    vmem = pl.BlockSpec(memory_space=pltpu.VMEM)
    rows = [w.shape[0] // devices for w in wholes]
    scratch = [pltpu.VMEM(w.shape, w.dtype) for w in wholes]
    scratch += [pltpu.VMEM((4, 4 * r, w.shape[1]), w.dtype) for r, w in zip(rows, wholes)]
    scratch += [pltpu.VMEM((2, 2 * r, w.shape[1]), w.dtype) for r, w in zip(rows, wholes)]
    scratch += [pltpu.VMEM((2, 4 * r, w.shape[1]), w.dtype) for r, w in zip(rows, wholes)]
    scratch += [pltpu.VMEM((4, r, w.shape[1]), w.dtype) for r, w in zip(rows, wholes)]
    scratch += [pltpu.VMEM((3, r, w.shape[1]), w.dtype) for r, w in zip(rows, wholes)]
    scratch += [pltpu.SemaphoreType.DMA((count, SCATTER_COPIES))] * 2
    return pl.pallas_call(
        functools.partial(scatter_kernel, count),
        out_shape=[jax.ShapeDtypeStruct((r, w.shape[1]), F32) for r, w in zip(rows, wholes)],
        in_specs=[vmem] * count, out_specs=[vmem] * count,
        scratch_shapes=scratch,
        compiler_params=pltpu.CompilerParams(
            collective_id=collective, has_side_effects=True, vmem_limit_bytes=60 << 20),
    )(*wholes)


GW = 128
PIX = 128


gamma_act = 1.7015
alpha_res = 0.2
beta_in = 0.9622504486493763
eps_std = 0.0001


def with_halo(block, sides, width):
    for axis, dim in sides:
        count = lax.axis_size(axis)
        forward = [(i, i + 1) for i in range(count - 1)]
        backward = [(target, source) for source, target in forward]
        low = lax.ppermute(
            lax.slice_in_dim(block, block.shape[dim] - width, None, axis=dim), axis, forward
        )
        high = lax.ppermute(lax.slice_in_dim(block, 0, width, axis=dim), axis, backward)
        block = jnp.concatenate([low, block, high], axis=dim)
    return block


def scaled_gelu(value):
    return gamma_act * jax.nn.gelu(value)


def input_act(value):
    return scaled_gelu(value) * beta_in


def double_sigmoid(value):
    return 2.0 * jax.nn.sigmoid(value)


def standard(kernel, gain):
    fan = kernel.shape[1]
    center = jnp.mean(kernel, axis=1, keepdims=True)
    spread_sq = jnp.mean(jnp.square(kernel - center), axis=1, keepdims=True)
    return gain[:, None] * (kernel - center) * lax.rsqrt(fan * spread_sq + eps_std)


def pull_back(func, value, cotan):
    return jax.vjp(func, value)[1](cotan)[0]


def columns(padded, wide, strip):
    blocks = padded.shape[0]
    groups = padded.shape[2] // GW
    places = jnp.arange(strip)
    pieces = []
    for step_row in (-1, 0, 1):
        for step_col in (-1, 0, 1):
            start_wide = 17 + step_row * 16 + step_col
            start_tall = 17 + step_row * 8 + step_col
            wide_part = lax.slice_in_dim(padded, start_wide, start_wide + strip, axis=1)
            tall_part = lax.slice_in_dim(padded, start_tall, start_tall + strip, axis=1)
            wide_ok = (places % 16 + step_col >= 0) & (places % 16 + step_col < 16)
            tall_ok = (places % 8 + step_col >= 0) & (places % 8 + step_col < 8)
            keep = jnp.where(wide[:, None], wide_ok[None, :], tall_ok[None, :])
            chosen = jnp.where(wide[:, None, None], wide_part, tall_part)
            chosen = jnp.where(keep[:, :, None], chosen, jnp.zeros_like(chosen))
            pieces.append(chosen.reshape(blocks, strip, groups, GW))
    stacked = jnp.stack(pieces, axis=3)
    return stacked.reshape(blocks * strip, groups, 9 * GW)


def forward_columns(field, wide):
    strip = field.shape[1]
    extended = with_halo(field, (("row", 1),), 16)
    return columns(jnp.pad(extended, ((0, 0), (1, 1), (0, 0))), wide, strip)


def backward_columns(field, wide):
    strip = field.shape[1]
    extended = with_halo(field, (("row", 1),), 16)
    return columns(jnp.pad(extended, ((0, 0), (1, 1), (0, 0))), wide, strip)


def spread(cols, kernel):
    groups = kernel.shape[0] // GW
    shaped = kernel.reshape(groups, GW, 9 * GW)
    result = jnp.einsum("rgk,gok->rgo", cols, shaped, preferred_element_type=jnp.float32)
    return result.reshape(cols.shape[0], groups * GW)


def flipped(kernel):
    groups = kernel.shape[0] // GW
    shaped = kernel.reshape(groups, GW, 9, GW)[:, :, ::-1, :]
    return jnp.transpose(shaped, (0, 3, 2, 1)).reshape(groups * GW, 9 * GW)


def kernel_grad(delta, cols):
    rows, groups, taps = cols.shape
    result = jnp.einsum(
        "rgo,rgk->gok", delta.reshape(rows, groups, GW), cols, preferred_element_type=jnp.float32
    )
    return result.reshape(groups * GW, taps)


def tuple_add(first, second):
    return tuple((left + right for left, right in zip(first, second)))


def micro_step(images_now, bucket_now, cotan_now, shared, skip, leader, count):
    (
        narrow_std,
        first_std,
        second_std,
        widen_std,
        squeeze_kernel,
        excite_kernel,
        narrow_bias,
        first_bias,
        second_bias,
        widen_bias,
        squeeze_bias,
        excite_bias,
    ) = shared
    blocks, strip, width = images_now.shape
    rows = blocks * strip
    wide = bucket_now == 0
    inputs = images_now.astype(jnp.float32)
    act_zero = input_act(inputs).astype(jnp.bfloat16).reshape(rows, width)
    pre_zero = jnp.einsum(
        "rd,md->rm", act_zero, narrow_std, preferred_element_type=jnp.float32
    ) + narrow_bias.astype(jnp.float32)
    act_one = scaled_gelu(pre_zero).astype(jnp.bfloat16).reshape(blocks, strip, -1)
    cols_one = forward_columns(act_one, wide)
    pre_one = spread(cols_one, first_std) + first_bias.astype(jnp.float32)
    act_two = scaled_gelu(pre_one).astype(jnp.bfloat16).reshape(blocks, strip, -1)
    cols_two = forward_columns(act_two, wide)
    pre_two = spread(cols_two, second_std) + second_bias.astype(jnp.float32)
    act_three = scaled_gelu(pre_two).astype(jnp.bfloat16)
    branch = jnp.einsum(
        "rm,dm->rd", act_three, widen_std, preferred_element_type=jnp.float32
    ) + widen_bias.astype(jnp.float32)
    branch_maps = branch.reshape(blocks, strip, width)
    pooled = (
        lax.psum(jnp.sum(branch_maps, axis=1).astype(jnp.bfloat16), "row").astype(jnp.float32) / PIX
    )
    pooled_low = pooled.astype(jnp.bfloat16)
    squeezed = jnp.einsum(
        "bd,md->bm", pooled_low, squeeze_kernel, preferred_element_type=jnp.float32
    ) + squeeze_bias.astype(jnp.float32)
    hidden_low = jax.nn.gelu(squeezed).astype(jnp.bfloat16)
    excited = jnp.einsum(
        "bm,dm->bd", hidden_low, excite_kernel, preferred_element_type=jnp.float32
    ) + excite_bias.astype(jnp.float32)
    gate = double_sigmoid(excited)
    output = (inputs + alpha_res * skip * (gate[:, None, :] * branch_maps)).astype(jnp.bfloat16)
    upstream = cotan_now.astype(jnp.float32)
    scaled = alpha_res * skip * upstream
    gate_grad = lax.psum(jnp.sum(scaled * branch_maps, axis=1).astype(jnp.bfloat16), "row").astype(
        jnp.float32
    )
    skip_part = jnp.sum(alpha_res * upstream * (gate[:, None, :] * branch_maps))
    excited_grad = pull_back(double_sigmoid, excited, gate_grad)
    excited_low = excited_grad.astype(jnp.bfloat16)
    excite_grad = jnp.einsum(
        "bd,bm->dm", excited_low, hidden_low, preferred_element_type=jnp.float32
    )
    hidden_grad = jnp.einsum(
        "bd,dm->bm", excited_low, excite_kernel, preferred_element_type=jnp.float32
    )
    squeezed_grad = pull_back(jax.nn.gelu, squeezed, hidden_grad)
    squeezed_low = squeezed_grad.astype(jnp.bfloat16)
    squeeze_grad = jnp.einsum(
        "bm,bd->md", squeezed_low, pooled_low, preferred_element_type=jnp.float32
    )
    pooled_grad = jnp.einsum(
        "bm,md->bd", squeezed_low, squeeze_kernel, preferred_element_type=jnp.float32
    )
    branch_grad = (scaled * gate[:, None, :] + pooled_grad[:, None, :] / PIX).reshape(rows, width)
    branch_low = branch_grad.astype(jnp.bfloat16)
    widen_grad = jnp.einsum("rd,rm->dm", branch_low, act_three, preferred_element_type=jnp.float32)
    three_grad = jnp.einsum("rd,dm->rm", branch_low, widen_std, preferred_element_type=jnp.float32)
    pre_two_grad = pull_back(scaled_gelu, pre_two, three_grad)
    two_low = pre_two_grad.astype(jnp.bfloat16)
    second_grad = kernel_grad(two_low, cols_two)
    two_grad = spread(
        backward_columns(two_low.reshape(blocks, strip, -1), wide), flipped(second_std)
    )
    pre_one_grad = pull_back(scaled_gelu, pre_one, two_grad)
    one_low = pre_one_grad.astype(jnp.bfloat16)
    first_grad = kernel_grad(one_low, cols_one)
    one_grad = spread(
        backward_columns(one_low.reshape(blocks, strip, -1), wide), flipped(first_std)
    )
    pre_zero_grad = pull_back(scaled_gelu, pre_zero, one_grad)
    zero_low = pre_zero_grad.astype(jnp.bfloat16)
    narrow_grad = jnp.einsum("rm,rd->md", zero_low, act_zero, preferred_element_type=jnp.float32)
    zero_grad = jnp.einsum("rm,md->rd", zero_low, narrow_std, preferred_element_type=jnp.float32)
    input_grad = (
        upstream + pull_back(input_act, inputs, zero_grad.reshape(blocks, strip, width))
    ).astype(jnp.bfloat16)
    grads = (
        narrow_grad,
        first_grad,
        second_grad,
        widen_grad,
        squeeze_grad * leader,
        excite_grad * leader,
        jnp.sum(pre_zero_grad, axis=0),
        jnp.sum(pre_one_grad, axis=0),
        jnp.sum(pre_two_grad, axis=0),
        jnp.sum(branch_grad, axis=0),
        jnp.sum(squeezed_grad, axis=0) * leader,
        jnp.sum(excited_grad, axis=0) * leader,
        jnp.full((count,), skip_part, jnp.float32),
    )
    return (output, input_grad, grads)


def body(
    images,
    bucket,
    cotangent,
    narrow_kernel,
    narrow_gain,
    narrow_bias,
    first_kernel,
    first_gain,
    first_bias,
    second_kernel,
    second_gain,
    second_bias,
    widen_kernel,
    widen_gain,
    widen_bias,
    squeeze_kernel,
    squeeze_bias,
    excite_kernel,
    excite_bias,
    skip_gain,
):
    count = lax.axis_size(("batch", "row"))
    leader = (lax.axis_index("row") == 0).astype(jnp.float32)
    skip = skip_gain.astype(jnp.float32)[0]
    narrow_std = standard(
        narrow_kernel.astype(jnp.float32), narrow_gain.astype(jnp.float32)
    ).astype(jnp.bfloat16)
    first_std = standard(first_kernel.astype(jnp.float32), first_gain.astype(jnp.float32)).astype(
        jnp.bfloat16
    )
    second_std = standard(
        second_kernel.astype(jnp.float32), second_gain.astype(jnp.float32)
    ).astype(jnp.bfloat16)
    widen_std = standard(widen_kernel.astype(jnp.float32), widen_gain.astype(jnp.float32)).astype(
        jnp.bfloat16
    )
    outputs = []
    input_grads = []
    axes = ("batch", "row")
    devices = lax.axis_size(axes)
    fits = lax.axis_size("batch") == 8 and lax.axis_size("row") == 4
    shards = (narrow_std, first_std, second_std, widen_std, squeeze_kernel, excite_kernel)
    if fits:
        kernels = gather_all(shards, devices, 0)
    else:
        kernels = [lax.all_gather(s, axes, axis=0, tiled=True) for s in shards]
    biases = [
        lax.all_gather(bias, axes, axis=0, tiled=True)
        for bias in (narrow_bias, first_bias, second_bias, widen_bias, squeeze_bias, excite_bias)
    ]
    shared = (*kernels, *biases)
    partial = None
    for number in range(images.shape[0]):
        output, input_grad, grads = micro_step(
            images[number], bucket[number], cotangent[number], shared, skip, leader, count
        )
        outputs.append(output)
        input_grads.append(input_grad)
        partial = grads if partial is None else tuple_add(partial, grads)
    if fits:
        low = [g.astype(BF) for g in partial[:6]]
        summed = [*scatter_all(low[:4], devices, 1), *scatter_all(low[4:], devices, 2)]
    else:
        summed = [
            lax.psum_scatter(g, axes, scatter_dimension=0, tiled=True) for g in partial[:6]
        ]
    summed += [lax.psum_scatter(g, axes, scatter_dimension=0, tiled=True) for g in partial[6:]]
    narrow_kernel_grad, narrow_gain_grad = jax.vjp(
        standard, narrow_kernel.astype(jnp.float32), narrow_gain.astype(jnp.float32)
    )[1](summed[0])
    first_kernel_grad, first_gain_grad = jax.vjp(
        standard, first_kernel.astype(jnp.float32), first_gain.astype(jnp.float32)
    )[1](summed[1])
    second_kernel_grad, second_gain_grad = jax.vjp(
        standard, second_kernel.astype(jnp.float32), second_gain.astype(jnp.float32)
    )[1](summed[2])
    widen_kernel_grad, widen_gain_grad = jax.vjp(
        standard, widen_kernel.astype(jnp.float32), widen_gain.astype(jnp.float32)
    )[1](summed[3])
    output_all = jnp.stack(outputs, axis=0)
    input_grad_all = jnp.stack(input_grads, axis=0)
    return (
        output_all,
        input_grad_all,
        narrow_kernel_grad,
        narrow_gain_grad,
        summed[6],
        first_kernel_grad,
        first_gain_grad,
        summed[7],
        second_kernel_grad,
        second_gain_grad,
        summed[8],
        widen_kernel_grad,
        widen_gain_grad,
        summed[9],
        summed[4],
        summed[10],
        summed[5],
        summed[11],
        summed[12],
    )


def solution(mesh):
    placed = (
        P(None, "batch", "row", None),
        P(None, "batch"),
        P(None, "batch", "row", None),
        P(("batch", "row"), None),
        P(("batch", "row")),
        P(("batch", "row")),
        P(("batch", "row"), None),
        P(("batch", "row")),
        P(("batch", "row")),
        P(("batch", "row"), None),
        P(("batch", "row")),
        P(("batch", "row")),
        P(("batch", "row"), None),
        P(("batch", "row")),
        P(("batch", "row")),
        P(("batch", "row"), None),
        P(("batch", "row")),
        P(("batch", "row"), None),
        P(("batch", "row")),
        P(),
    )
    return jax.shard_map(
        body,
        mesh=mesh,
        in_specs=placed,
        out_specs=(
            P(None, "batch", "row", None),
            P(None, "batch", "row", None),
            P(("batch", "row"), None),
            P(("batch", "row")),
            P(("batch", "row")),
            P(("batch", "row"), None),
            P(("batch", "row")),
            P(("batch", "row")),
            P(("batch", "row"), None),
            P(("batch", "row")),
            P(("batch", "row")),
            P(("batch", "row"), None),
            P(("batch", "row")),
            P(("batch", "row")),
            P(("batch", "row"), None),
            P(("batch", "row")),
            P(("batch", "row"), None),
            P(("batch", "row")),
            P(),
        ),
        check_vma=False,
    )
```

```python
import functools
import math
import types

import jax
import jax.numpy as jnp
from jax import lax
from jax.experimental import pallas as pl
from jax.experimental.pallas import tpu as pltpu
from jax.sharding import PartitionSpec as P

MESH = pl.DeviceIdType.MESH
BF = jnp.bfloat16
F32 = jnp.float32

GW = 128
PIX = 128
TAPS = 9
gamma_act = 1.7015
alpha_res = 0.2
beta_in = 0.9622504486493763
eps_std = 0.0001
tanh_scale = math.sqrt(2.0 / math.pi)
tanh_cube = 0.044715

NN = ((1,), (0,))
NT = ((1,), (1,))
TN = ((0,), (0,))


def dot(left, right, dims):
    return lax.dot_general(left, right, (dims, ((), ())), preferred_element_type=F32)


def place():
    return lax.axis_index("batch"), lax.axis_index("row")


def flip(value, bit):
    return lax.bitwise_xor(value, jnp.int32(bit))


def tile(index, size):
    return pl.ds(pl.multiple_of(index * size, size), size)


def greet(everywhere):
    b, z = place()
    barrier = pltpu.get_barrier_semaphore()
    for bit in (1, 2, 3):
        pl.semaphore_signal(barrier, inc=1, device_id=(b, flip(z, bit)), device_id_type=MESH)
    if everywhere:
        for bit in (1, 2, 4):
            pl.semaphore_signal(barrier, inc=1, device_id=(flip(b, bit), z), device_id_type=MESH)
    pl.semaphore_wait(barrier, 6 if everywhere else 3)


class Transfer:
    def __init__(self, send, recv):
        self.send, self.recv, self.copies = send, recv, {}

    def copy(self, key, src, dst, device):
        made = pltpu.make_async_remote_copy(
            src_ref=src, dst_ref=dst, send_sem=self.send.at[key], recv_sem=self.recv.at[key],
            device_id=device, device_id_type=MESH)
        made.start()
        self.copies[key] = made

    def arrived(self, *keys):
        for key in keys:
            self.copies[key].wait_recv()

    def close(self):
        for made in self.copies.values():
            made.wait_send()


class Gather(Transfer):
    def __init__(self, slots, whole, send, recv, halves=True, block=None):
        super().__init__(send, recv)
        self.slots, self.whole, self.halves = slots, whole, halves
        self.rows = slots.shape[1]
        self.block = 4 * self.rows if block is None else block
        self.half = self.block // 2

    def at(self, index, start=0, size=None):
        size = self.block if size is None else size
        return self.whole.at[pl.ds(pl.multiple_of(index * self.block + start, 8 if self.rows == 8 else 16), size)]

    def along_row(self):
        b, z = place()
        for j in (1, 2, 3):
            self.copy(j - 1, self.slots.at[z], self.slots.at[z], (b, flip(z, j)))

    def assemble(self):
        b, z = place()
        base = pl.multiple_of(b * self.block, 16)
        if self.rows % 16 == 0:
            for r in range(4):
                self.whole[pl.ds(base + r * self.rows, self.rows)] = self.slots[r]
        else:
            for r in (0, 2):
                pair = jnp.concatenate([self.slots[r].astype(F32), self.slots[r + 1].astype(F32)], axis=0)
                self.whole[pl.ds(base + r * self.rows, 2 * self.rows)] = pair.astype(self.whole.dtype)

    def own_block(self):
        b, z = place()
        self.arrived(0, 1, 2)
        self.assemble()
        own = self.at(b)
        self.copy(3, own, own, (flip(b, 2), z))
        self.copy(4, own, own, (flip(b, 4), z))
        self.copy(5, own, own, (flip(b, 1), z))

    def onward(self):
        b, z = place()
        self.arrived(3)
        low = self.at(flip(b, 2), 0, self.half) if self.halves else self.at(flip(b, 2))
        self.copy(6, low, low, (flip(b, 4), z))
        near = self.at(flip(b, 2))
        self.copy(8, near, near, (flip(b, 1), z))
        self.arrived(4)
        if self.halves:
            high = self.at(flip(b, 4), self.half, self.half)
            self.copy(7, high, high, (flip(b, 2), z))
        near = self.at(flip(b, 4))
        self.copy(9, near, near, (flip(b, 1), z))

    def corner(self):
        b, z = place()
        self.arrived(6)
        if self.halves:
            self.arrived(7)
        far = self.at(flip(b, 6))
        self.copy(10, far, far, (flip(b, 1), z))

    def ready(self):
        self.arrived(5, 8, 9, 10)


class Factors(Gather):
    def assemble(self):
        b, z = place()
        width = self.slots.shape[2]
        columns = []
        for q in range(4):
            rows = [self.slots[r].astype(F32)[4 * q:4 * q + 4] for r in range(4)]
            columns.append(jnp.concatenate(rows, axis=0))
        self.whole[pl.ds(pl.multiple_of(b * 16, 16), 16)] = jnp.concatenate(columns, axis=1).astype(BF)


class Scatter(Transfer):
    def __init__(self, whole, mate, diagonal, sides, pieces, landed, send, recv):
        super().__init__(send, recv)
        self.whole, self.mate, self.diagonal, self.sides = whole, mate, diagonal, sides
        self.pieces, self.landed = pieces, landed
        self.rows = pieces.shape[1]
        self.block = 4 * self.rows
        self.half = self.block // 2

    def at(self, index, start=0, size=None):
        size = self.block if size is None else size
        return self.whole.at[pl.ds(pl.multiple_of(index * self.block + start, 16), size)]

    def to_mate(self):
        b, z = place()
        for k, q in enumerate((6, 2, 4, 0)):
            self.copy(k, self.at(flip(b, 1 ^ q)), self.mate.at[k], (flip(b, 1), z))

    def add(self, index, start, size, ref):
        where = pl.ds(pl.multiple_of(index * self.block + start, 16), size)
        total = self.whole[where].astype(F32) + ref[...].astype(F32)
        self.whole[where] = total.astype(self.whole.dtype)

    def diagonals(self):
        b, z = place()
        self.arrived(0)
        self.add(flip(b, 6), 0, self.block, self.mate.at[0])
        self.copy(4, self.at(flip(b, 6), 0, self.half), self.diagonal.at[0], (flip(b, 4), z))
        self.copy(5, self.at(flip(b, 6), self.half, self.half), self.diagonal.at[1], (flip(b, 2), z))
        self.arrived(1)
        self.add(flip(b, 2), 0, self.block, self.mate.at[1])
        self.arrived(2)
        self.add(flip(b, 4), 0, self.block, self.mate.at[2])
        self.arrived(3)
        self.add(b, 0, self.block, self.mate.at[3])

    def to_sides(self):
        b, z = place()
        self.arrived(4)
        self.add(flip(b, 2), 0, self.half, self.diagonal.at[0])
        self.copy(6, self.at(flip(b, 2)), self.sides.at[0], (flip(b, 2), z))
        self.arrived(5)
        self.add(flip(b, 4), self.half, self.half, self.diagonal.at[1])
        self.copy(7, self.at(flip(b, 4)), self.sides.at[1], (flip(b, 4), z))

    def along_row(self):
        b, z = place()
        self.arrived(6, 7)
        step = 1 if self.rows % 16 == 0 else 2
        size = step * self.rows
        for r in range(0, 4, step):
            start = r * self.rows
            part = self.whole[pl.ds(pl.multiple_of(b * self.block + start, 16), size)].astype(F32)
            for side in (0, 1):
                part += self.sides[side, start:start + size].astype(F32)
            for k in range(step):
                self.pieces[r + k] = part[k * self.rows:(k + 1) * self.rows].astype(self.pieces.dtype)
        for j in (1, 2, 3):
            self.copy(7 + j, self.pieces.at[flip(z, j)], self.landed.at[j - 1], (b, flip(z, j)))

    def total(self):
        b, z = place()
        result = self.pieces[z].astype(F32)
        for j in (1, 2, 3):
            self.arrived(7 + j)
            result += self.landed[j - 1].astype(F32)
        return result


class Halo:
    def __init__(self, field, send, recv, blocks):
        self.field, self.send, self.recv, self.blocks = field, send, recv, blocks

    def made(self, part, way):
        b, z = place()
        images = pl.ds(part * self.blocks, self.blocks)
        source, target, step = ((32, 0, 1), (16, 48, -1))[way]
        return pltpu.make_async_remote_copy(
            src_ref=self.field.at[images, pl.ds(source, 16)], dst_ref=self.field.at[images, pl.ds(target, 16)],
            send_sem=self.send.at[part, way], recv_sem=self.recv.at[part, way],
            device_id=(b, z + step), device_id_type=MESH)

    def each(self, part, low, high, act):
        b, z = place()

        @pl.when(z < 3)
        def _():
            act(self.made(part, low))

        @pl.when(z > 0)
        def _():
            act(self.made(part, high))

    def start(self, part):
        self.each(part, 0, 1, lambda made: made.start())

    def arrived(self, part):
        self.each(part, 1, 0, lambda made: made.wait_recv())

    def close(self, part):
        self.each(part, 0, 1, lambda made: made.wait_send())


def act_only(value):
    inner = jnp.tanh(tanh_scale * value * (1.0 + tanh_cube * (value * value)))
    return (0.5 * gamma_act) * value * (1.0 + inner)


def gelu_pair(value, scale):
    square = value * value
    inner = jnp.tanh(tanh_scale * value * (1.0 + tanh_cube * square))
    half = 0.5 + 0.5 * inner
    slope = half + (0.5 * tanh_scale) * value * (1.0 - inner * inner) * (1.0 + (3.0 * tanh_cube) * square)
    return scale * value * half, scale * slope


def column(row, count):
    lanes = lax.broadcasted_iota(jnp.int32, (count, 128), 1)
    ups = lax.broadcasted_iota(jnp.int32, (count, 128), 0)
    return jnp.sum(jnp.where(lanes == ups, row, 0.0), axis=1, keepdims=True)


def as_row(col, count):
    lanes = lax.broadcasted_iota(jnp.int32, (count, 128), 1)
    ups = lax.broadcasted_iota(jnp.int32, (count, 128), 0)
    return jnp.sum(jnp.where(lanes == ups, col, 0.0), axis=0, keepdims=True)


def centred(kernel_ref):
    kernel = kernel_ref[...].astype(F32)
    fan = kernel.shape[1]
    center = kernel - jnp.mean(kernel, axis=1, keepdims=True)
    spread = jnp.mean(center * center, axis=1, keepdims=True)
    return center, lax.rsqrt(fan * spread + eps_std)


def standard(kernel_ref, gain):
    center, scale = centred(kernel_ref)
    return gain * center * scale


def standard_back(kernel_ref, gain, cotan):
    center, scale = centred(kernel_ref)
    along = jnp.sum(cotan * center, axis=1, keepdims=True)
    mean = jnp.mean(cotan, axis=1, keepdims=True)
    kernel_grad = (gain * scale) * (cotan - mean) - (gain * along * scale * scale * scale) * center
    return kernel_grad, along * scale


def owners(devices, share, width):
    place_of = lax.broadcasted_iota(jnp.int32, (128, width), 1).astype(F32)
    within = place_of - share * jnp.floor((place_of + 0.5) * (1.0 / share))
    slot = lax.broadcasted_iota(jnp.int32, (128, width), 0).astype(F32)
    pick = jnp.where(within == slot, 1.0, 0.0).astype(BF)
    index = lax.broadcasted_iota(jnp.int32, (devices, width), 1)
    owner = lax.broadcasted_iota(jnp.int32, (devices, width), 0)
    mine = (index >= owner * share) & (index < owner * share + share)
    return pick, mine


def from_shares(shares, share, width):
    pick, mine = owners(shares.shape[0], share, width)
    spread = dot(shares.astype(BF), pick, NN)
    return jnp.sum(jnp.where(mine, spread, 0.0), axis=0, keepdims=True)


def to_shares(row, devices, share):
    pick, mine = owners(devices, share, row.shape[1])
    masked = jnp.where(mine, row, 0.0)
    upper = masked.astype(BF)
    lower = (masked - upper.astype(F32)).astype(BF)
    return dot(upper, pick, NT) + dot(lower, pick, NT)


def build_columns(field, cols, bucket, part, blocks, reverse):
    width = field.shape[2]

    def body(i, carry):
        image = part * blocks + i
        value = field[image].astype(F32)
        size = jnp.where(bucket[part, i] == 0, 16, 8)
        place_in = jnp.bitwise_and(lax.broadcasted_iota(jnp.int32, (64, width), 0), size - 1)
        left = jnp.where(place_in != 0, pltpu.roll(value, 1, 0), 0.0)
        right = jnp.where(place_in != size - 1, pltpu.roll(value, 63, 0), 0.0)
        wide = jnp.full((32, width), size, jnp.int32) == 16
        for step_col, moved in ((-1, left), (0, value), (1, right)):
            for step_row in (-1, 0, 1):
                if step_row == 0:
                    tap = moved[16:48]
                elif step_row == -1:
                    tap = jnp.where(wide, moved[0:32], moved[8:40])
                else:
                    tap = jnp.where(wide, moved[32:64], moved[24:56])
                t = (step_row + 1) * 3 + step_col + 1
                t = 8 - t if reverse else t
                tap = tap.astype(BF)
                rows = pl.ds(pl.multiple_of(image * 32, 32), 32)
                for g in range(width // GW):
                    cols[g, rows, t * GW:(t + 1) * GW] = tap[:, g * GW:(g + 1) * GW]
        return carry

    lax.fori_loop(0, blocks, body, 0)


def narrow_part(ns, part):
    rows = tile(part, ns.strip)
    images = pl.ds(part * ns.blocks, ns.blocks)

    def body(n, carry):
        lanes = tile(n, 256)
        value = dot(ns.act0[rows, :], ns.w[0][lanes, :], NT) + ns.brow[0:1, lanes]
        act, slope = gelu_pair(value, gamma_act)
        ns.slope0[rows, lanes] = slope.astype(BF)
        ns.ext1[images, 16:48, lanes] = act.reshape(ns.blocks, 32, 256).astype(BF)
        return carry

    lax.fori_loop(0, ns.mid // 256, body, 0)


def group_part(ns, part, which, target, slope_ref):
    rows = tile(part, ns.strip)
    images = pl.ds(part * ns.blocks, ns.blocks)

    def body(g, carry):
        lanes = tile(g, GW)
        value = dot(ns.cols[g, rows, :], ns.w[which][lanes, :], NT) + ns.brow[which:which + 1, lanes]
        act, slope = gelu_pair(value, gamma_act)
        slope_ref[rows, lanes] = slope.astype(BF)
        if target is ns.act3:
            target[rows, lanes] = act.astype(BF)
        else:
            target[images, 16:48, lanes] = act.reshape(ns.blocks, 32, GW).astype(BF)
        return carry

    lax.fori_loop(0, ns.mid // GW, body, 0)


def widen_part(ns, part):
    rows = tile(part, ns.strip)

    def body(n, carry):
        lanes = tile(n, 256)
        branch = dot(ns.act3[rows, :], ns.w[3][lanes, :], NT) + ns.brow[3:4, lanes]
        ns.out[rows, lanes] = branch.astype(BF)
        upstream = ns.cotangent[rows, lanes].astype(F32)
        images = tile(part, ns.blocks)
        ns.sums[0, images, lanes] = jnp.sum(branch.reshape(ns.blocks, 32, 256), axis=1)
        ns.sums[1, images, lanes] = jnp.sum((branch * upstream).reshape(ns.blocks, 32, 256), axis=1)
        return carry

    lax.fori_loop(0, ns.width // 256, body, 0)


def send_sums(ns):
    b, z = place()
    half = ns.width // 2
    for r in range(4):
        parts = [ns.sums[kind, 4 * r:4 * r + 4, side * half:(side + 1) * half] for kind in (0, 1) for side in (0, 1)]
        ns.shared_out[r] = jnp.concatenate(parts, axis=0).astype(BF)
    for j in (1, 2, 3):
        ns.pool.copy(j - 1, ns.shared_out.at[flip(z, j)], ns.shared_in.at[j - 1], (b, flip(z, j)))


def excite_images(ns):
    b, z = place()
    total = ns.shared_out[z].astype(F32)
    for j in (1, 2, 3):
        ns.pool.arrived(j - 1)
        total += ns.shared_in[j - 1].astype(F32)
    pad = jnp.zeros((12, ns.width), F32)
    pooled = jnp.concatenate([total[0:4], total[4:8]], axis=1) * (1.0 / PIX)
    along = jnp.concatenate([total[8:12], total[12:16]], axis=1)
    pooled = jnp.concatenate([pooled, pad], axis=0).astype(BF)
    along = alpha_res * jnp.concatenate([along, pad], axis=0)
    squeezed = dot(pooled, ns.w[4][...], NT) + ns.brow[4:5, 0:ns.mid]
    hidden, slope = gelu_pair(squeezed, 1.0)
    hidden = hidden.astype(BF)
    excited = dot(hidden, ns.w[5][...], NT) + ns.brow[5:6, :]
    sigmoid = jax.nn.sigmoid(excited)
    gate = 2.0 * sigmoid
    excited_grad = (ns.skip * along) * (gate * (1.0 - sigmoid))
    excited_low = excited_grad.astype(BF)
    squeezed_grad = dot(excited_low, ns.w[5][...], NN) * slope
    squeezed_low = squeezed_grad.astype(BF)
    pooled_grad = dot(squeezed_low, ns.w[4][...], NN) * (1.0 / PIX)
    half = ns.width // 2
    parts = [value[0:4, side * half:(side + 1) * half] for value in (gate, pooled_grad) for side in (0, 1)]
    ns.shared_back[z] = jnp.concatenate(parts, axis=0).astype(BF)
    for j in (1, 2, 3):
        ns.back.copy(j - 1, ns.shared_back.at[z], ns.shared_back.at[z], (b, flip(z, j)))
    ns.bias_sums[4:5, 0:ns.mid] = jnp.sum(squeezed_grad, axis=0, keepdims=True)
    ns.bias_sums[5:6, :] = jnp.sum(excited_grad, axis=0, keepdims=True)
    ns.bias_sums[6:7, :] = jnp.full((1, ns.width), jnp.sum(gate * along), F32)
    combined = jnp.concatenate(
        [value.astype(F32)[0:4] for value in (excited_low, hidden, squeezed_low, pooled)], axis=1)
    quarter = combined.shape[1] // 4
    ns.factor_slots[z] = jnp.concatenate(
        [combined[:, q * quarter:(q + 1) * quarter] for q in range(4)], axis=0).astype(BF)
    ns.factors.along_row()


def take_gates(ns):
    ns.back.arrived(0, 1, 2)
    half = ns.width // 2
    for r in range(4):
        value = ns.shared_back[r].astype(F32)
        for k in range(4):
            ns.gates[k // 2, 4 * r:4 * r + 4, (k % 2) * half:(k % 2 + 1) * half] = value[4 * k:4 * k + 4]


def branch_back(ns):
    ns.widen_sum[...] = jnp.zeros_like(ns.widen_sum)

    def body(i, carry):
        rows = tile(i, 32)
        gate, pooled_grad = ns.gates[0, pl.ds(i, 1), :], ns.gates[1, pl.ds(i, 1), :]
        upstream = ns.cotangent[rows, :].astype(F32)
        strong = (alpha_res * ns.skip) * gate
        grad = upstream * strong + pooled_grad
        ns.out[rows, :] = (ns.images[rows, :].astype(F32) + strong * ns.out[rows, :].astype(F32)).astype(BF)
        ns.dx[rows, :] = grad.astype(BF)
        ns.widen_sum[...] += jnp.sum(grad.reshape(4, 8, ns.width), axis=0)
        return carry

    lax.fori_loop(0, ns.images.shape[0] // 32, body, 0)
    ns.bias_sums[3:4, :] = jnp.sum(ns.widen_sum[...], axis=0, keepdims=True)


def widen_grad(ns):
    def body(n, carry):
        lanes = tile(n, 256)
        ns.g[3][lanes, :] = dot(ns.dx[:, lanes], ns.act3[...], TN).astype(BF)
        return carry

    lax.fori_loop(0, ns.width // 256, body, 0)


def widen_back(ns, part):
    rows = tile(part, ns.strip)
    images = pl.ds(part * ns.blocks, ns.blocks)

    def body(n, carry):
        lanes = tile(n, 256)
        grad = dot(ns.dx[rows, :], ns.w[3][:, lanes], NN) * ns.slope2[rows, lanes].astype(F32)
        ns.bias_sums[2:3, lanes] += jnp.sum(grad, axis=0, keepdims=True)
        ns.low2[images, 16:48, lanes] = grad.reshape(ns.blocks, 32, 256).astype(BF)
        return carry

    lax.fori_loop(0, ns.mid // 256, body, 0)


def group_grad(ns, low, which):
    total = ns.images.shape[0]

    def body(g, carry):
        lanes = tile(g, GW)
        delta = low[:, 16:48, lanes].reshape(total, GW)
        ns.g[which][lanes, :] = dot(delta, ns.cols[g], TN).astype(BF)
        return carry

    lax.fori_loop(0, ns.mid // GW, body, 0)


def group_back(ns, part, which, slope_ref, target):
    rows = tile(part, ns.strip)
    images = pl.ds(part * ns.blocks, ns.blocks)

    def body(g, carry):
        lanes = tile(g, GW)
        stacked = jnp.concatenate(
            [ns.w[which][lanes, t * GW:(t + 1) * GW] for t in range(TAPS)], axis=0)
        grad = dot(ns.cols[g, rows, :], stacked, NN) * slope_ref[rows, lanes].astype(F32)
        ns.bias_sums[which - 1:which, lanes] += jnp.sum(grad, axis=0, keepdims=True)
        if target is ns.act3:
            target[rows, lanes] = grad.astype(BF)
        else:
            target[images, 16:48, lanes] = grad.reshape(ns.blocks, 32, GW).astype(BF)
        return carry

    lax.fori_loop(0, ns.mid // GW, body, 0)


def narrow_grad(ns):
    wide = ns.width // 512

    def body(k, carry):
        up, lanes = tile(k // wide, 256), tile(k % wide, 512)
        ns.g[0][up, lanes] = dot(ns.act3[:, up], ns.act0[:, lanes], TN).astype(BF)
        return carry

    lax.fori_loop(0, ns.mid // 256 * wide, body, 0)


def input_back(ns, part):
    rows = tile(part, ns.strip)

    def body(n, carry):
        lanes = tile(n, 256)
        grad = dot(ns.act3[rows, :], ns.w[0][:, lanes], NN)
        slope = gelu_pair(ns.images[rows, lanes].astype(F32), gamma_act * beta_in)[1]
        ns.dx[rows, lanes] = (ns.cotangent[rows, lanes].astype(F32) + grad * slope).astype(BF)
        return carry

    lax.fori_loop(0, ns.width // 256, body, 0)


def excite_grads(ns):
    b, z = place()
    device = b * 4 + z
    values = ns.factor_rows[...]
    at = [0, ns.width, ns.width + ns.mid, ns.width + 2 * ns.mid, 2 * ns.width + 2 * ns.mid]
    excited, hidden, squeezed, pooled = [values[:, at[k]:at[k + 1]] for k in range(4)]
    for own, other, share, target in (
        (excited, hidden, ns.shares[5], ns.grad_out[5]),
        (squeezed, pooled, ns.shares[4], ns.grad_out[4]),
    ):
        span = -(-share // 16) * 16
        wide = own.shape[1]
        lanes = lax.broadcasted_iota(jnp.int32, (span, wide), 1)
        ups = lax.broadcasted_iota(jnp.int32, (span, wide), 0)
        pick = jnp.where(lanes == ups + device * share, 1.0, 0.0).astype(BF)
        mine = dot(pick, own, NT).astype(BF)
        target[...] = dot(mine, other, NN)[:share]


def block_kernel(names, settings, *refs):
    ns = types.SimpleNamespace(**dict(zip(names, refs)), **settings)
    fits = ns.fits
    ns.strip = ns.images.shape[0] // ns.micro
    ns.blocks = ns.strip // 32
    ns.width = ns.images.shape[1]
    ns.w = [getattr(ns, f"w{k}") for k in range(6)]
    ns.g = [getattr(ns, f"g{k}", None) for k in range(4)]
    ns.mid = ns.w[0].shape[0]
    b, z = place()
    parts = range(ns.micro)
    fields = (ns.ext1, ns.ext2, ns.low2, ns.low1)
    for field in fields:
        edge = jnp.zeros((field.shape[0], 16, field.shape[2]), BF)
        field[:, 0:16, :] = edge
        field[:, 48:64, :] = edge
    ns.bias_sums[...] = jnp.zeros_like(ns.bias_sums)
    greet(fits)
    halo1, halo2, halo3, halo4 = [
        Halo(field, ns.halo_send.at[k], ns.halo_recv.at[k], ns.blocks) for k, field in enumerate(fields)]
    ns.pool = Transfer(ns.se_send.at[0], ns.se_recv.at[0])
    ns.back = Transfer(ns.se_send.at[1], ns.se_recv.at[1])
    ns.factors = Factors(
        ns.factor_slots, ns.factor_rows, ns.gather_send.at[7], ns.gather_recv.at[7], halves=False, block=16)
    jobs = []
    if fits:
        ns.gains = [column(ns.vecs[8 + k:9 + k, :], ns.shares[k]) for k in range(4)]
        ns.bias_slots[z] = ns.vecs[0:8, :]
        jobs.append(Gather(ns.bias_slots, ns.bias_rows, ns.gather_send.at[6], ns.gather_recv.at[6]))
        jobs[0].along_row()
        for k in range(6):
            slots, shard = getattr(ns, f"slots{k}"), getattr(ns, f"shard{k}")
            slots[z] = standard(shard, ns.gains[k]).astype(BF) if k < 4 else shard[...]
            jobs.append(Gather(slots, ns.w[k], ns.gather_send.at[k], ns.gather_recv.at[k]))
            jobs[-1].along_row()

    def pump(own=None, onward=None, corner=None, ready=None):
        if fits:
            if own is not None:
                jobs[own].own_block()
            if onward is not None:
                jobs[onward].onward()
            if corner is not None:
                jobs[corner].corner()
            if ready is not None:
                jobs[ready].ready()

    pump(own=0)
    pump(own=1)

    def first_act(i, carry):
        rows = tile(i, 32)
        ns.act0[rows, :] = (act_only(ns.images[rows, :].astype(F32)) * beta_in).astype(BF)
        return carry

    lax.fori_loop(0, ns.images.shape[0] // 32, first_act, 0)
    pump(onward=0, own=2)
    pump(onward=1, corner=0, own=3)
    pump(onward=2, corner=1, ready=0)
    if fits:
        for k in range(6):
            share = ns.shares[k]
            width = share * ns.devices
            ns.brow[k:k + 1, 0:width] = from_shares(ns.bias_rows[pl.ds(k, ns.devices, stride=8), :], share, width)
        ns.skip = ns.vecs[6:7, 0:1]
    else:
        ns.skip = ns.brow[6:7, 0:1]
    pump(ready=1)
    for part in parts:
        narrow_part(ns, part)
        halo1.start(part)
    pump(own=4, onward=3, corner=2, ready=2)
    for part in parts:
        halo1.arrived(part)
        build_columns(ns.ext1, ns.cols, ns.bucket, part, ns.blocks, False)
        group_part(ns, part, 1, ns.ext2, ns.slope1)
        halo2.start(part)
    pump(own=5, onward=4, corner=3, ready=3)
    for part in parts:
        halo2.arrived(part)
        build_columns(ns.ext2, ns.cols, ns.bucket, part, ns.blocks, False)
        group_part(ns, part, 2, ns.act3, ns.slope2)
    pump(own=6, onward=5, corner=4, ready=4)
    for part in parts:
        widen_part(ns, part)
    send_sums(ns)
    pump(onward=6, corner=5, ready=5)
    pump(corner=6, ready=6)
    excite_images(ns)
    for job in jobs:
        job.close()
    take_gates(ns)
    branch_back(ns)
    scatters = [None] * 5
    if fits:
        for k in range(5):
            refs_of = [getattr(ns, f"{name}{k}") for name in ("mate", "diagonal", "sides", "pieces", "landed")]
            scatters[k] = Scatter(
                ns.g[k] if k < 4 else ns.bias_parts, *refs_of, ns.scatter_send.at[k], ns.scatter_recv.at[k])

    def push(*steps):
        if fits:
            for name, k in steps:
                getattr(scatters[k], name)()

    widen_grad(ns)
    push(("to_mate", 3))
    for part in parts:
        widen_back(ns, part)
        halo3.start(part)
    push(("diagonals", 3))
    group_grad(ns, ns.low2, 2)
    push(("to_mate", 2), ("to_sides", 3))
    if fits:
        ns.factors.own_block()
    for part in parts:
        halo3.arrived(part)
        build_columns(ns.low2, ns.cols, ns.bucket, part, ns.blocks, True)
        group_back(ns, part, 2, ns.slope1, ns.low1)
        halo4.start(part)
    push(("diagonals", 2), ("along_row", 3))
    for part in parts:
        build_columns(ns.ext1, ns.cols, ns.bucket, part, ns.blocks, False)
    group_grad(ns, ns.low1, 1)
    push(("to_mate", 1), ("to_sides", 2))
    if fits:
        ns.factors.onward()
    for part in parts:
        halo4.arrived(part)
        build_columns(ns.low1, ns.cols, ns.bucket, part, ns.blocks, True)
        group_back(ns, part, 1, ns.slope0, ns.act3)
    push(("diagonals", 1))
    narrow_grad(ns)
    push(("to_mate", 0))
    if fits:
        for k in range(6):
            row = ns.bias_sums[k:k + 1, 0:ns.shares[k] * ns.devices]
            ns.bias_parts[pl.ds(k, ns.devices, stride=8), :] = to_shares(row, ns.devices, ns.shares[k])
        ns.bias_parts[pl.ds(6, ns.devices, stride=8), :] = jnp.broadcast_to(
            ns.bias_sums[6:7, 0:128], (ns.devices, 128))
        ns.bias_parts[pl.ds(7, ns.devices, stride=8), :] = jnp.zeros((ns.devices, 128), F32)
    push(("to_mate", 4), ("along_row", 2), ("to_sides", 1))
    for part in parts:
        input_back(ns, part)
        if part == 0:
            push(("diagonals", 0), ("diagonals", 4))
    push(("along_row", 1), ("to_sides", 0), ("to_sides", 4))
    if fits:
        ns.factors.corner()

        def settle(k):
            kernel_grad, gain_grad = standard_back(getattr(ns, f"shard{k}"), ns.gains[k], scatters[k].total())
            ns.grad_out[k][...] = kernel_grad
            ns.gain_out[k][...] = as_row(gain_grad, ns.shares[k])[:, 0:ns.shares[k]]

        for k in (3, 2):
            settle(k)
        ns.factors.ready()
        excite_grads(ns)
        push(("along_row", 0), ("along_row", 4))
        settle(1)
        settle(0)
        bias_total = scatters[4].total()
        for k in range(6):
            ns.bias_out[k][...] = bias_total[k:k + 1, 0:ns.shares[k]]
        ns.skip_out[...] = bias_total[6:7, 0:1]
        for job in scatters:
            job.close()
    else:
        ns.factor_out[...] = ns.factor_slots[z]
        ns.factors.arrived(0, 1, 2)
        ns.bias_sums_out[...] = ns.bias_sums[...]
    ns.factors.close()
    for halo in (halo1, halo2, halo3, halo4):
        for part in parts:
            halo.close(part)
    ns.pool.close()
    ns.back.close()


def run_block(images, bucket, cotangent, kernels, vectors, devices, fits):
    micro, blocks, strip, width = images.shape
    total = micro * blocks * strip
    mid = kernels[0].shape[0] * (devices if fits else 1)
    shares = [k.shape[0] // (1 if fits else devices) for k in kernels]
    vmem = pl.BlockSpec(memory_space=pltpu.VMEM)
    smem = pl.BlockSpec(memory_space=pltpu.SMEM)
    names, specs, args = [], [], []

    def operand(name, value, spec=vmem):
        names.append(name)
        specs.append(spec)
        args.append(value)

    operand("bucket", bucket, smem)
    operand("images", images.reshape(total, width))
    operand("cotangent", cotangent.reshape(total, width))
    for k, kernel in enumerate(kernels):
        operand(f"shard{k}" if fits else f"w{k}", kernel)
    operand("vecs" if fits else "brow", vectors)
    outs = []

    def result(name, shape, dtype):
        names.append(name)
        outs.append(jax.ShapeDtypeStruct(shape, dtype))

    result("out", (total, width), BF)
    result("dx", (total, width), BF)
    if fits:
        for k in range(6):
            result(f"grad_out{k}", kernels[k].shape, F32)
        for k in range(4):
            result(f"gain_out{k}", (1, shares[k]), F32)
        for k in range(6):
            result(f"bias_out{k}", (1, shares[k]), F32)
        result("skip_out", (1, 1), F32)
    else:
        for k in range(4):
            result(f"g{k}", kernels[k].shape, BF)
        result("factor_out", (16, (width + mid) // 2), BF)
        result("bias_sums_out", (8, width), F32)
    scratch = []

    def keep(name, shape, dtype):
        names.append(name)
        scratch.append(pltpu.VMEM(shape, dtype))

    images_here = micro * blocks
    whole_shapes = [(s * devices, k.shape[1]) for s, k in zip(shares, kernels)]
    if fits:
        for k, shape in enumerate(whole_shapes):
            keep(f"w{k}", shape, BF)
            keep(f"slots{k}", (4, shares[k], shape[1]), BF)
        keep("bias_slots", (4, 8, 128), F32)
        keep("bias_rows", (devices * 8, 128), F32)
        keep("brow", (8, width), F32)
        for k in (1, 2):
            keep(f"g{k}", whole_shapes[k], BF)
        keep("bias_parts", (devices * 8, 128), F32)
        for k in range(5):
            share, span, dtype = (shares[k], whole_shapes[k][1], BF) if k < 4 else (8, 128, F32)
            keep(f"mate{k}", (4, 4 * share, span), dtype)
            keep(f"diagonal{k}", (2, 2 * share, span), dtype)
            keep(f"sides{k}", (2, 4 * share, span), dtype)
            keep(f"pieces{k}", (4, share, span), dtype)
            keep(f"landed{k}", (3, share, span), dtype)
    keep("act0", (total, width), BF)
    for name in ("slope0", "slope1", "slope2", "act3"):
        keep(name, (total, mid), BF)
    for name in ("ext1", "ext2", "low2", "low1"):
        keep(name, (images_here, 64, mid), BF)
    keep("cols", (mid // GW, total, TAPS * GW), BF)
    keep("sums", (2, images_here, width), F32)
    keep("gates", (2, images_here, width), F32)
    keep("widen_sum", (8, width), F32)
    keep("bias_sums", (8, width), F32)
    keep("shared_out", (4, 16, width // 2), BF)
    keep("shared_in", (3, 16, width // 2), BF)
    keep("shared_back", (4, 16, width // 2), BF)
    keep("factor_slots", (4, 16, (width + mid) // 2), BF)
    keep("factor_rows", (devices // 4 * 16, 2 * (width + mid)), BF)
    for name, shape in (
        ("gather_send", (8, 11)), ("gather_recv", (8, 11)), ("scatter_send", (5, 11)), ("scatter_recv", (5, 11)),
        ("halo_send", (4, micro, 2)), ("halo_recv", (4, micro, 2)), ("se_send", (2, 3)), ("se_recv", (2, 3)),
    ):
        names.append(name)
        scratch.append(pltpu.SemaphoreType.DMA(shape))
    settings = dict(fits=fits, devices=devices, micro=micro, shares=shares)

    def kernel(*refs):
        by_name = dict(zip(names, refs))
        extra = {}
        if fits:
            extra["grad_out"] = [by_name[f"grad_out{k}"] for k in range(6)]
            extra["gain_out"] = [by_name[f"gain_out{k}"] for k in range(4)]
            extra["bias_out"] = [by_name[f"bias_out{k}"] for k in range(6)]
            extra["g0"], extra["g3"] = by_name["w4"], by_name["w5"]
        block_kernel(list(by_name) + list(extra), settings, *by_name.values(), *extra.values())

    return pl.pallas_call(
        kernel,
        out_shape=outs,
        in_specs=specs,
        out_specs=[vmem] * len(outs),
        scratch_shapes=scratch,
        compiler_params=pltpu.CompilerParams(
            collective_id=0, has_side_effects=True, vmem_limit_bytes=63 << 20),
    )(*args)


def scaled_std(kernel, gain):
    fan = kernel.shape[1]
    center = kernel - jnp.mean(kernel, axis=1, keepdims=True)
    spread = jnp.mean(jnp.square(center), axis=1, keepdims=True)
    return gain[:, None] * center * lax.rsqrt(fan * spread + eps_std)


def padded(vector):
    return jnp.pad(vector.astype(F32), (0, 128 - vector.shape[0]))


def body(
    images, bucket, cotangent,
    narrow_kernel, narrow_gain, narrow_bias, first_kernel, first_gain, first_bias,
    second_kernel, second_gain, second_bias, widen_kernel, widen_gain, widen_bias,
    squeeze_kernel, squeeze_bias, excite_kernel, excite_bias, skip_gain,
):
    axes = ("batch", "row")
    devices = lax.axis_size(axes)
    fits = lax.axis_size("batch") == 8
    shape = images.shape
    kernels = [narrow_kernel, first_kernel, second_kernel, widen_kernel]
    maps = [squeeze_kernel, excite_kernel]
    gains = [narrow_gain, first_gain, second_gain, widen_gain]
    biases = [narrow_bias, first_bias, second_bias, widen_bias, squeeze_bias, excite_bias]
    if fits:
        none = jnp.zeros((1,), F32)
        rows = biases + [skip_gain, none] + gains + [none] * 4
        vectors = jnp.stack([padded(row) for row in rows])
        got = run_block(images, bucket, cotangent, kernels + maps, vectors, devices, True)
        output, input_grad = got[0], got[1]
        kernel_grads, gain_grads = got[2:8], [g.reshape(-1) for g in got[8:12]]
        bias_grads, skip_grad = [g.reshape(-1) for g in got[12:18]], got[18].reshape(1)
    else:
        gather = functools.partial(lax.all_gather, axis_name=axes, axis=0, tiled=True)
        scatter = functools.partial(lax.psum_scatter, axis_name=axes, scatter_dimension=0, tiled=True)
        floats = [(k.astype(F32), g.astype(F32)) for k, g in zip(kernels, gains)]
        wholes = [gather(scaled_std(k, g).astype(BF)) for k, g in floats] + [gather(m) for m in maps]
        width = shape[3]
        rows = [gather(bias).astype(F32) for bias in biases] + [skip_gain.astype(F32), jnp.zeros((1,), F32)]
        vectors = jnp.stack([jnp.pad(row, (0, width - row.shape[0])) for row in rows])
        got = run_block(images, bucket, cotangent, wholes, vectors, devices, False)
        output, input_grad = got[0], got[1]
        totals = [scatter(g.astype(F32)) for g in got[2:6]]
        pulled = [jax.vjp(scaled_std, k, g)[1](t) for (k, g), t in zip(floats, totals)]
        kernel_grads, gain_grads = [p[0] for p in pulled], [p[1] for p in pulled]
        sums = got[7]
        bias_grads = [scatter(sums[k, :wholes[k].shape[0]]) for k in range(6)]
        skip_grad = lax.psum(sums[6, 0:1], axes)
        mid = wholes[0].shape[0]
        packed = gather(got[6]).reshape(devices, 4, 4, -1)
        values = jnp.transpose(packed, (0, 2, 1, 3)).reshape(devices * 4, -1)
        excited, hidden, squeezed, pooled = jnp.split(values, [width, width + mid, width + 2 * mid], axis=1)
        device = lax.axis_index(axes)
        for own, other, kernel in ((squeezed, pooled, squeeze_kernel), (excited, hidden, excite_kernel)):
            share = kernel.shape[0]
            mine = lax.dynamic_slice_in_dim(own, device * share, share, axis=1)
            kernel_grads.append(dot(mine, other, TN))
    return (
        output.reshape(shape), input_grad.reshape(shape),
        kernel_grads[0], gain_grads[0], bias_grads[0],
        kernel_grads[1], gain_grads[1], bias_grads[1],
        kernel_grads[2], gain_grads[2], bias_grads[2],
        kernel_grads[3], gain_grads[3], bias_grads[3],
        kernel_grads[4], bias_grads[4], kernel_grads[5], bias_grads[5],
        skip_grad,
    )


def solution(mesh):
    maps, shared = P(None, "batch", "row", None), P(("batch", "row"))
    rows = P(("batch", "row"), None)
    weight = (rows, shared, shared)
    return jax.shard_map(
        body,
        mesh=mesh,
        in_specs=(maps, P(None, "batch"), maps, *weight * 4, rows, shared, rows, shared, P()),
        out_specs=(maps, maps, *weight * 4, rows, shared, rows, shared, P()),
        check_vma=False,
    )
```

```python
import functools
import math
import types

import jax
import jax.numpy as jnp
from jax import lax
from jax.experimental import pallas as pl
from jax.experimental.pallas import tpu as pltpu
from jax.sharding import PartitionSpec as P

MESH = pl.DeviceIdType.MESH
BF = jnp.bfloat16
F32 = jnp.float32

GW = 128
PIX = 128
TAPS = 9
gamma_act = 1.7015
alpha_res = 0.2
beta_in = 0.9622504486493763
eps_std = 0.0001
tanh_scale = math.sqrt(2.0 / math.pi)
tanh_cube = 0.044715

NN = ((1,), (0,))
NT = ((1,), (1,))
TN = ((0,), (0,))


def dot(left, right, dims):
    return lax.dot_general(left, right, (dims, ((), ())), preferred_element_type=F32)


def place():
    return lax.axis_index("batch"), lax.axis_index("row")


def flip(value, bit):
    return lax.bitwise_xor(value, jnp.int32(bit))


def tile(index, size):
    return pl.ds(pl.multiple_of(index * size, size), size)


def greet(everywhere):
    b, z = place()
    barrier = pltpu.get_barrier_semaphore()
    for bit in (1, 2, 3):
        pl.semaphore_signal(barrier, inc=1, device_id=(b, flip(z, bit)), device_id_type=MESH)
    if everywhere:
        for bit in (1, 2, 4):
            pl.semaphore_signal(barrier, inc=1, device_id=(flip(b, bit), z), device_id_type=MESH)
    pl.semaphore_wait(barrier, 6 if everywhere else 3)


class Transfer:
    def __init__(self, send, recv):
        self.send, self.recv, self.copies = send, recv, {}

    def copy(self, key, src, dst, device):
        made = pltpu.make_async_remote_copy(
            src_ref=src, dst_ref=dst, send_sem=self.send.at[key], recv_sem=self.recv.at[key],
            device_id=device, device_id_type=MESH)
        made.start()
        self.copies[key] = made

    def arrived(self, *keys):
        for key in keys:
            self.copies[key].wait_recv()

    def close(self):
        for made in self.copies.values():
            made.wait_send()


class Gather(Transfer):
    def __init__(self, slots, whole, send, recv):
        super().__init__(send, recv)
        self.slots, self.whole = slots, whole
        self.rows = slots.shape[1]
        self.block = 4 * self.rows
        self.half = self.block // 2

    def at(self, index, start=0, size=None):
        size = self.block if size is None else size
        return self.whole.at[pl.ds(pl.multiple_of(index * self.block + start, 8 if self.rows == 8 else 16), size)]

    def along_row(self):
        b, z = place()
        for j in (1, 2, 3):
            self.copy(j - 1, self.slots.at[z], self.slots.at[z], (b, flip(z, j)))

    def assemble(self):
        b, z = place()
        base = pl.multiple_of(b * self.block, 16)
        if self.rows % 16 == 0:
            for r in range(4):
                self.whole[pl.ds(base + r * self.rows, self.rows)] = self.slots[r]
        else:
            for r in (0, 2):
                pair = jnp.concatenate([self.slots[r].astype(F32), self.slots[r + 1].astype(F32)], axis=0)
                self.whole[pl.ds(base + r * self.rows, 2 * self.rows)] = pair.astype(self.whole.dtype)

    def own_block(self):
        b, z = place()
        self.arrived(0, 1, 2)
        self.assemble()
        own = self.at(b)
        self.copy(3, own, own, (flip(b, 2), z))
        self.copy(4, own, own, (flip(b, 4), z))
        self.copy(5, own, own, (flip(b, 1), z))

    def onward(self):
        b, z = place()
        self.arrived(3)
        low = self.at(flip(b, 2), 0, self.half)
        self.copy(6, low, low, (flip(b, 4), z))
        near = self.at(flip(b, 2))
        self.copy(8, near, near, (flip(b, 1), z))
        self.arrived(4)
        high = self.at(flip(b, 4), self.half, self.half)
        self.copy(7, high, high, (flip(b, 2), z))
        near = self.at(flip(b, 4))
        self.copy(9, near, near, (flip(b, 1), z))

    def corner(self):
        b, z = place()
        self.arrived(6, 7)
        far = self.at(flip(b, 6))
        self.copy(10, far, far, (flip(b, 1), z))

    def ready(self):
        self.arrived(5, 8, 9, 10)


class PlaneGather(Transfer):
    def __init__(self, whole, send, recv, bit):
        super().__init__(send, recv)
        self.whole, self.bit = whole, bit

    def copy_block(self, key, index, bit):
        b, z = place()
        block = self.whole.at[index]
        self.copy(key, block, block, (flip(b, bit), z))

    def own_block(self):
        b, z = place()
        for key, bit in ((0, 2), (1, 4), (2, 1)):
            self.copy_block(key, b, bit)

    def onward(self):
        b, z = place()
        for key, bit in ((0, 2), (1, 4)):
            self.arrived(key)
            if self.bit != bit:
                self.copy_block(6, flip(b, bit), self.bit)
            self.copy_block(3 + key, flip(b, bit), 1)

    def corner(self):
        b, z = place()
        self.arrived(6)
        self.copy_block(5, flip(b, 6), 1)

    def ready(self):
        self.arrived(2, 3, 4, 5)


class Scatter(Transfer):
    def __init__(self, whole, mate, diagonal, sides, pieces, landed, send, recv):
        super().__init__(send, recv)
        self.whole, self.mate, self.diagonal, self.sides = whole, mate, diagonal, sides
        self.pieces, self.landed = pieces, landed
        self.rows = pieces.shape[1]
        self.block = 4 * self.rows
        self.half = self.block // 2

    def at(self, index, start=0, size=None):
        size = self.block if size is None else size
        return self.whole.at[pl.ds(pl.multiple_of(index * self.block + start, 16), size)]

    def to_mate(self):
        b, z = place()
        for k, q in enumerate((6, 2, 4, 0)):
            self.copy(k, self.at(flip(b, 1 ^ q)), self.mate.at[k], (flip(b, 1), z))

    def add(self, index, start, size, ref):
        where = pl.ds(pl.multiple_of(index * self.block + start, 16), size)
        total = self.whole[where].astype(F32) + ref[...].astype(F32)
        self.whole[where] = total.astype(self.whole.dtype)

    def diagonals(self):
        b, z = place()
        x_mate, y_mate = (flip(b, 2), z), (flip(b, 4), z)
        low, high = pl.ds(0, self.half), pl.ds(self.half, self.half)
        self.arrived(0)
        self.add(flip(b, 6), 0, self.block, self.mate.at[0])
        self.copy(4, self.at(flip(b, 6), 0, self.half), self.diagonal.at[0], y_mate)
        self.copy(5, self.at(flip(b, 6), self.half, self.half), self.diagonal.at[1], x_mate)
        self.arrived(1)
        self.add(flip(b, 2), 0, self.block, self.mate.at[1])
        self.copy(6, self.at(flip(b, 2), self.half, self.half), self.sides.at[0, high], x_mate)
        self.arrived(2)
        self.add(flip(b, 4), 0, self.block, self.mate.at[2])
        self.copy(7, self.at(flip(b, 4), 0, self.half), self.sides.at[1, low], y_mate)

    def to_sides(self):
        b, z = place()
        low, high = pl.ds(0, self.half), pl.ds(self.half, self.half)
        self.arrived(4)
        self.add(flip(b, 2), 0, self.half, self.diagonal.at[0])
        self.copy(8, self.at(flip(b, 2), 0, self.half), self.sides.at[0, low], (flip(b, 2), z))
        self.arrived(5)
        self.add(flip(b, 4), self.half, self.half, self.diagonal.at[1])
        self.copy(9, self.at(flip(b, 4), self.half, self.half), self.sides.at[1, high], (flip(b, 4), z))

    def along_row(self):
        b, z = place()
        self.arrived(3, 6, 7, 8, 9)
        step = 1 if self.rows % 16 == 0 else 2
        size = step * self.rows
        for r in range(0, 4, step):
            start = r * self.rows
            part = self.whole[pl.ds(pl.multiple_of(b * self.block + start, 16), size)].astype(F32)
            for held in (self.mate.at[3], self.sides.at[0], self.sides.at[1]):
                part += held[start:start + size].astype(F32)
            for k in range(step):
                self.pieces[r + k] = part[k * self.rows:(k + 1) * self.rows].astype(self.pieces.dtype)
        for j in (1, 2, 3):
            self.copy(9 + j, self.pieces.at[flip(z, j)], self.landed.at[j - 1], (b, flip(z, j)))

    def total(self):
        b, z = place()
        result = self.pieces[z].astype(F32)
        for j in (1, 2, 3):
            self.arrived(9 + j)
            result += self.landed[j - 1].astype(F32)
        return result


class Halo:
    def __init__(self, field, send, recv, blocks):
        self.field, self.send, self.recv, self.blocks = field, send, recv, blocks

    def made(self, part, way):
        b, z = place()
        images = pl.ds(part * self.blocks, self.blocks)
        source, target, step = ((32, 0, 1), (16, 48, -1))[way]
        return pltpu.make_async_remote_copy(
            src_ref=self.field.at[images, pl.ds(source, 16)], dst_ref=self.field.at[images, pl.ds(target, 16)],
            send_sem=self.send.at[part, way], recv_sem=self.recv.at[part, way],
            device_id=(b, z + step), device_id_type=MESH)

    def each(self, part, low, high, act):
        b, z = place()

        @pl.when(z < 3)
        def _():
            act(self.made(part, low))

        @pl.when(z > 0)
        def _():
            act(self.made(part, high))

    def clear_ends(self):
        b, z = place()
        edge = jnp.zeros((self.field.shape[0], 16, self.field.shape[2]), BF)

        @pl.when(z == 0)
        def _():
            self.field[:, 0:16, :] = edge

        @pl.when(z == 3)
        def _():
            self.field[:, 48:64, :] = edge

    def start(self, part):
        self.each(part, 0, 1, lambda made: made.start())

    def arrived(self, part):
        self.each(part, 1, 0, lambda made: made.wait_recv())

    def close(self, part):
        self.each(part, 0, 1, lambda made: made.wait_send())


def act_only(value):
    inner = jnp.tanh(tanh_scale * value * (1.0 + tanh_cube * (value * value)))
    return (0.5 * gamma_act) * value * (1.0 + inner)


def gelu_pair(value, scale):
    square = value * value
    inner = jnp.tanh(tanh_scale * value * (1.0 + tanh_cube * square))
    half = 0.5 + 0.5 * inner
    slope = half + (0.5 * tanh_scale) * value * (1.0 - inner * inner) * (1.0 + (3.0 * tanh_cube) * square)
    return scale * value * half, scale * slope


def column(row, count):
    lanes = lax.broadcasted_iota(jnp.int32, (count, 128), 1)
    ups = lax.broadcasted_iota(jnp.int32, (count, 128), 0)
    return jnp.sum(jnp.where(lanes == ups, row, 0.0), axis=1, keepdims=True)


def as_row(col, count):
    lanes = lax.broadcasted_iota(jnp.int32, (count, 128), 1)
    ups = lax.broadcasted_iota(jnp.int32, (count, 128), 0)
    return jnp.sum(jnp.where(lanes == ups, col, 0.0), axis=0, keepdims=True)


def centred(kernel_ref):
    kernel = kernel_ref[...].astype(F32)
    fan = kernel.shape[1]
    center = kernel - jnp.mean(kernel, axis=1, keepdims=True)
    spread = jnp.mean(center * center, axis=1, keepdims=True)
    return center, lax.rsqrt(fan * spread + eps_std)


def standard(kernel_ref, gain):
    center, scale = centred(kernel_ref)
    return gain * center * scale


def standard_back(kernel_ref, gain, cotan):
    center, scale = centred(kernel_ref)
    along = jnp.sum(cotan * center, axis=1, keepdims=True)
    mean = jnp.mean(cotan, axis=1, keepdims=True)
    kernel_grad = (gain * scale) * (cotan - mean) - (gain * along * scale * scale * scale) * center
    return kernel_grad, along * scale


def remainder(value, size):
    count = jnp.floor((value + 0.5) * (1.0 / size))
    return value - size * count, count


def owners(devices, share, width, row=None):
    index = lax.broadcasted_iota(jnp.int32, (128, width), 1).astype(F32)
    slot = lax.broadcasted_iota(jnp.int32, (128, width), 0).astype(F32)
    pick = jnp.where(remainder(index, share)[0] == slot, 1.0, 0.0).astype(BF)
    index = lax.broadcasted_iota(jnp.int32, (devices, width), 1)
    owner = lax.broadcasted_iota(jnp.int32, (devices, width), 0)
    start = owner * share if row is None else lax.shift_right_logical(owner, 2) * share
    mine = (index >= start) & (index < start + share)
    if row is not None:
        mine = mine & (jnp.bitwise_and(owner, 3) == row)
    return pick, mine


def from_shares(shares, share, width, row=None):
    pick, mine = owners(shares.shape[0], share, width, row)
    spread = dot(shares.astype(BF), pick, NN)
    return jnp.sum(jnp.where(mine, spread, 0.0), axis=0, keepdims=True)


def to_shares(vector, devices, share, row=None):
    pick, mine = owners(devices, share, vector.shape[1], row)
    masked = jnp.where(mine, vector, 0.0)
    upper = masked.astype(BF)
    lower = (masked - upper.astype(F32)).astype(BF)
    return dot(upper, pick, NT) + dot(lower, pick, NT)


def row_order(groups, share):
    total = 4 * groups * share
    within, row = remainder(lax.broadcasted_iota(jnp.int32, (total, 1), 0).astype(F32), groups * share)
    entry, group = remainder(within, share)
    target = (group * 4 + row) * share + entry
    index = lax.broadcasted_iota(jnp.int32, (total, total), 1).astype(F32)
    return jnp.where(index == target, 1.0, 0.0).astype(BF)


def build_columns(field, cols, bucket, part, blocks, reverse):
    width = field.shape[2]

    def body(i, carry):
        image = part * blocks + i
        value = field[image].astype(F32)
        size = jnp.where(bucket[part, i] == 0, 16, 8)
        place_in = jnp.bitwise_and(lax.broadcasted_iota(jnp.int32, (64, width), 0), size - 1)
        left = jnp.where(place_in != 0, pltpu.roll(value, 1, 0), 0.0)
        right = jnp.where(place_in != size - 1, pltpu.roll(value, 63, 0), 0.0)
        wide = jnp.full((32, width), size, jnp.int32) == 16
        for step_col, moved in ((-1, left), (0, value), (1, right)):
            for step_row in (-1, 0, 1):
                if step_row == 0:
                    tap = moved[16:48]
                elif step_row == -1:
                    tap = jnp.where(wide, moved[0:32], moved[8:40])
                else:
                    tap = jnp.where(wide, moved[32:64], moved[24:56])
                t = (step_row + 1) * 3 + step_col + 1
                t = 8 - t if reverse else t
                tap = tap.astype(BF)
                rows = pl.ds(pl.multiple_of(image * 32, 32), 32)
                for g in range(width // GW):
                    cols[g, rows, t * GW:(t + 1) * GW] = tap[:, g * GW:(g + 1) * GW]
        return carry

    lax.fori_loop(0, blocks, body, 0)


def split_dot(left, pieces):
    total, at = None, 0
    for piece in pieces:
        part = dot(left[:, at:at + piece.shape[1]], piece[...], NT)
        total, at = part if total is None else total + part, at + piece.shape[1]
    return total


def narrow_part(ns, part):
    rows = tile(part, ns.strip)
    images = pl.ds(part * ns.blocks, ns.blocks)

    def body(n, carry):
        lanes = tile(n, 256)
        value = split_dot(ns.act0.at[rows], [w.at[lanes] for w in ns.w[0]]) + ns.brow[0:1, lanes]
        act, slope = gelu_pair(value, gamma_act)
        ns.slope0[rows, lanes] = slope.astype(BF)
        ns.ext1[images, 16:48, lanes] = act.reshape(ns.blocks, 32, 256).astype(BF)
        return carry

    lax.fori_loop(0, ns.mid // 256, body, 0)


def group_part(ns, part, which, cols, target, slope_ref):
    rows = tile(part, ns.strip)
    images = pl.ds(part * ns.blocks, ns.blocks)

    def body(g, carry):
        lanes = tile(g, GW)
        value = dot(cols[g, rows, :], ns.w[which][0][lanes, :], NT) + ns.brow[which:which + 1, lanes]
        act, slope = gelu_pair(value, gamma_act)
        slope_ref[rows, lanes] = slope.astype(BF)
        low = act.astype(BF)
        if target is ns.act3:
            target[rows, lanes] = low
            ns.third_sums[tile(part, ns.blocks), lanes] = jnp.sum(
                low.astype(F32).reshape(ns.blocks, 32, GW), axis=1)
        else:
            target[images, 16:48, lanes] = low.reshape(ns.blocks, 32, GW)
        return carry

    lax.fori_loop(0, ns.mid // GW, body, 0)


def widen_part(ns, part):
    rows = tile(part, ns.strip)

    def body(n, carry):
        lanes = tile(n, 256)
        branch = split_dot(ns.act3.at[rows], [w.at[lanes] for w in ns.w[3]]) + ns.brow[3:4, lanes]
        ns.out[rows, lanes] = branch.astype(BF)
        upstream = ns.cotangent[rows, lanes].astype(F32)
        ns.along_sums[tile(part, ns.blocks), lanes] = jnp.sum(
            (branch * upstream).reshape(ns.blocks, 32, 256), axis=1)
        return carry

    lax.fori_loop(0, ns.width // 256, body, 0)


def to_row(ns, group, source, target):
    b, z = place()
    for j in (1, 2, 3):
        group.copy(j - 1, source(flip(z, j)), target(j - 1), (b, flip(z, j)))


def to_all(ns, group, slots):
    b, z = place()
    to_row(ns, group, lambda r: slots.at[z], lambda j: slots.at[z])


def row_pieces(ns, value):
    share = ns.shares[5]
    for r in range(4):
        pieces = [value[:, (4 * p + r) * share:(4 * p + r + 1) * share] for p in range(ns.devices // 4)]
        yield r, jnp.concatenate(pieces, axis=1)


def send_third(ns):
    b, z = place()
    ns.third_slots[z] = ns.third_sums[...].astype(BF)
    to_all(ns, ns.third, ns.third_slots)


def send_along(ns):
    for r, value in row_pieces(ns, ns.along_sums[...]):
        ns.along_out[r] = value.astype(BF)
    to_row(ns, ns.along, lambda r: ns.along_out.at[r], lambda j: ns.along_in.at[j])


def prepare_maps(ns):
    ns.order[...] = row_order(ns.devices // 4, ns.shares[4])
    half = ns.mid // 2
    if ns.fits:
        share = ns.shares[4]
        for side, whole in enumerate(ns.squeeze_halves):
            span = whole.shape[2]
            for p in range(0, ns.devices // 4, 2):
                pair = jnp.concatenate([whole[p].astype(F32), whole[p + 1].astype(F32)], axis=0).astype(BF)
                ns.squeeze[p * share:(p + 2) * share, side * span:(side + 1) * span] = pair
        sides = [whole[...].reshape(-1, half) for whole in ns.excite_halves]
    else:
        sides = [ns.excite_whole[:, side * half:(side + 1) * half] for side in (0, 1)]
    moved = sum(dot(value, ns.order[:, side * half:(side + 1) * half], NT) for side, value in enumerate(sides))
    ns.excite[...] = moved.astype(BF)


def total_of(slots):
    return sum(slots[r].astype(F32) for r in range(4))


def received(own, landed):
    b, z = place()
    return own[z].astype(F32) + sum(landed[j].astype(F32) for j in range(3))


def squeeze_images(ns):
    b, z = place()
    quarter, span = ns.squeeze.shape[0], ns.excite.shape[0]
    ns.third.arrived(0, 1, 2)
    third = total_of(ns.third_slots)
    upper = third.astype(BF)
    lower = (third - upper.astype(F32)).astype(BF)
    both = split_dot(jnp.concatenate([upper, lower], axis=0), ns.w[3])
    count = third.shape[0]
    pooled = ((both[:count] + both[count:]) * (1.0 / PIX) + ns.brow[3:4, :]).astype(BF)
    squeezed = dot(pooled, ns.squeeze[...], NT) + ns.brow[4:5, 0:quarter]
    hidden, slope = gelu_pair(squeezed, 1.0)
    ns.squeeze_slope[...] = slope
    ns.hidden_slots[z] = hidden.astype(BF)
    to_all(ns, ns.hidden, ns.hidden_slots)
    ns.factor_rows[b, :, ns.factor_at[2]:ns.factor_at[3]] = pooled
    ns.factor_rows[b, :, ns.factor_at[3]:ns.factor_at[4]] = upper


def excite_images(ns):
    b, z = place()
    span = ns.excite.shape[0]
    ns.hidden.arrived(0, 1, 2)
    hidden = jnp.concatenate([ns.hidden_slots[r].astype(F32) for r in range(4)], axis=1).astype(BF)
    ns.sigmoid[...] = jax.nn.sigmoid(dot(hidden, ns.excite[...], NT) + ns.brow[5:6, 0:span])
    ns.gate_slots[z] = (2.0 * ns.sigmoid[...]).astype(BF)
    to_all(ns, ns.gate, ns.gate_slots)
    ns.factor_rows[b, :, ns.factor_at[1]:ns.factor_at[2]] = dot(hidden, ns.order[...], NN).astype(BF)


def take_gates(ns):
    share = ns.shares[5]
    ns.gate.arrived(0, 1, 2)
    slots = [ns.gate_slots[r].astype(F32) for r in range(4)]
    pieces = [slots[r][:, p * share:(p + 1) * share] for p in range(ns.devices // 4) for r in range(4)]
    ns.gates[...] = jnp.concatenate(pieces, axis=1)


def excite_back(ns):
    b, z = place()
    quarter, span = ns.squeeze.shape[0], ns.excite.shape[0]
    ns.along.arrived(0, 1, 2)
    along = alpha_res * received(ns.along_out, ns.along_in)
    sigmoid = ns.sigmoid[...]
    gate = 2.0 * sigmoid
    excited_grad = (ns.skip * along) * (gate * (1.0 - sigmoid))
    excited_low = excited_grad.astype(BF)
    partial = dot(excited_low, ns.excite[...], NN)
    for r in range(4):
        ns.hidden_out[r] = partial[:, r * quarter:(r + 1) * quarter].astype(BF)
    to_row(ns, ns.hidden_back, lambda r: ns.hidden_out.at[r], lambda j: ns.hidden_in.at[j])
    ns.bias_sums[5:6, 0:span] = jnp.sum(excited_grad, axis=0, keepdims=True)
    ns.bias_sums[6:7, :] = jnp.full((1, ns.width), jnp.sum(gate * along), F32)
    ns.factor_rows[b, :, 0:span] = excited_low


def squeeze_back(ns):
    b, z = place()
    quarter = ns.squeeze.shape[0]
    ns.hidden_back.arrived(0, 1, 2)
    squeezed_grad = received(ns.hidden_out, ns.hidden_in) * ns.squeeze_slope[...]
    squeezed_low = squeezed_grad.astype(BF)
    pooled_grad = dot(squeezed_low, ns.squeeze[...], NN) * (1.0 / PIX)
    low = pooled_grad.astype(BF)
    ns.back_slots[z] = jnp.concatenate([dot(low, w[...], NN) for w in ns.w[3]], axis=1).astype(BF)
    to_all(ns, ns.back, ns.back_slots)
    for r, value in row_pieces(ns, pooled_grad):
        ns.pooled_out[r] = value.astype(BF)
    to_row(ns, ns.pooled_back, lambda r: ns.pooled_out.at[r], lambda j: ns.pooled_in.at[j])
    ns.pooled_sum[...] = PIX * jnp.sum(pooled_grad, axis=0, keepdims=True)
    ns.bias_sums[4:5, 0:quarter] = jnp.sum(squeezed_grad, axis=0, keepdims=True)
    ns.late_rows[b, :, ns.excite.shape[0]:] = squeezed_low


def take_pooled(ns):
    b, z = place()
    ns.pooled_back.arrived(0, 1, 2)
    ns.late_rows[b, :, 0:ns.excite.shape[0]] = received(ns.pooled_out, ns.pooled_in).astype(BF)


def branch_back(ns, part):
    def body(i, carry):
        image = part * ns.blocks + i
        rows = tile(image, 32)
        grad = ns.cotangent[rows, :].astype(F32) * ((alpha_res * ns.skip) * ns.gates[pl.ds(image, 1), :])
        ns.dx[rows, :] = grad.astype(BF)
        ns.widen_sum[...] += jnp.sum(grad.reshape(4, 8, ns.width), axis=0)
        return carry

    lax.fori_loop(0, ns.blocks, body, 0)


def add_branch(ns):
    def body(image, carry):
        rows = tile(image, 32)
        strong = (alpha_res * ns.skip) * ns.gates[pl.ds(image, 1), :]
        ns.out[rows, :] = (ns.images[rows, :].astype(F32) + strong * ns.out[rows, :].astype(F32)).astype(BF)
        return carry

    lax.fori_loop(0, ns.images.shape[0] // 32, body, 0)


def widen_grad(ns):
    def body(n, carry):
        lanes = tile(n, 256)
        ns.g[3][0][lanes, :] = dot(ns.dx[:, lanes], ns.act3[...], TN).astype(BF)
        return carry

    lax.fori_loop(0, ns.width // 256, body, 0)


def widen_back(ns, part):
    rows = tile(part, ns.strip)
    images = pl.ds(part * ns.blocks, ns.blocks)
    for piece, w in enumerate(ns.w[3]):
        span = min(256, w.shape[1])

        def body(n, carry):
            here = tile(n, span)
            lanes = pl.ds(pl.multiple_of(piece * w.shape[1] + n * span, span), span)
            grad = dot(ns.dx[rows, :], w[:, here], NN)
            ns.ext2[images, 16:48, lanes] = grad.reshape(ns.blocks, 32, span).astype(BF)
            return carry

        lax.fori_loop(0, w.shape[1] // span, body, 0)


def third_back(ns, part):
    def body(i, carry):
        image = part * ns.blocks + i
        rows = tile(image, 32)
        grad = ns.ext2[image, 16:48, :].astype(F32) + ns.third_pooled[pl.ds(image, 1), :]
        grad = grad * ns.slope2[rows, :].astype(F32)
        ns.ext2[image, 16:48, :] = grad.astype(BF)
        ns.second_sum[...] += jnp.sum(grad.reshape(4, 8, ns.mid), axis=0)
        return carry

    lax.fori_loop(0, ns.blocks, body, 0)


def group_grad(ns, low, cols, which):
    total = ns.images.shape[0]

    def body(g, carry):
        lanes = tile(g, GW)
        delta = low[:, 16:48, lanes].reshape(total, GW)
        ns.g[which][0][lanes, :] = dot(delta, cols[g], TN).astype(BF)
        return carry

    lax.fori_loop(0, ns.mid // GW, body, 0)


def group_back(ns, part, which, slope_ref, target):
    rows = tile(part, ns.strip)
    images = pl.ds(part * ns.blocks, ns.blocks)

    def body(g, carry):
        lanes = tile(g, GW)
        stacked = jnp.concatenate(
            [ns.w[which][0][lanes, t * GW:(t + 1) * GW] for t in range(TAPS)], axis=0)
        grad = dot(ns.cols[g, rows, :], stacked, NN) * slope_ref[rows, lanes].astype(F32)
        ns.bias_sums[which - 1:which, lanes] += jnp.sum(grad, axis=0, keepdims=True)
        if target is ns.act3:
            target[rows, lanes] = grad.astype(BF)
        else:
            target[images, 16:48, lanes] = grad.reshape(ns.blocks, 32, GW).astype(BF)
        return carry

    lax.fori_loop(0, ns.mid // GW, body, 0)


def narrow_grad(ns, piece):
    target = ns.g[0][piece]
    span = target.shape[1]

    def body(k, carry):
        up = tile(k, 256)
        target[up, :] = dot(ns.act3[:, up], ns.act0[:, piece * span:(piece + 1) * span], TN).astype(BF)
        return carry

    lax.fori_loop(0, ns.mid // 256, body, 0)


def input_back(ns, part):
    rows = tile(part, ns.strip)
    for piece, w in enumerate(ns.w[0]):
        span = w.shape[1]

        def body(n, carry):
            here = tile(n, 256)
            lanes = pl.ds(pl.multiple_of(piece * span + n * 256, 256), 256)
            grad = dot(ns.act3[rows, :], w[:, here], NN)
            slope = gelu_pair(ns.images[rows, lanes].astype(F32), gamma_act * beta_in)[1]
            ns.dx[rows, lanes] = (ns.cotangent[rows, lanes].astype(F32) + grad * slope).astype(BF)
            return carry

        lax.fori_loop(0, span // 256, body, 0)


def excite_grads(ns):
    b, z = place()
    values = ns.factor_rows[...].reshape(-1, ns.factor_rows.shape[2])
    excited, hidden, pooled, third = [
        values[:, start:stop] for start, stop in zip(ns.factor_at[:-1], ns.factor_at[1:])]
    late = ns.late_rows[...].reshape(-1, ns.late_rows.shape[2])
    pooled_grad, squeezed = late[:, :ns.excite.shape[0]], late[:, ns.excite.shape[0]:]
    results = []
    for own, other, share in (
        (excited, hidden, ns.shares[5]), (squeezed, pooled, ns.shares[4]), (pooled_grad, third, ns.shares[5]),
    ):
        height = -(-share // 16) * 16
        lanes = lax.broadcasted_iota(jnp.int32, (height, own.shape[1]), 1)
        ups = lax.broadcasted_iota(jnp.int32, (height, own.shape[1]), 0)
        pick = jnp.where(lanes == ups + b * share, 1.0, 0.0).astype(BF)
        mine = dot(pick, own, NT).astype(BF)
        results.append(dot(mine, other, NN)[:share])
    ns.grad_out[5][...], ns.grad_out[4][...] = results[:2]
    return results[2]


def block_kernel(names, settings, *refs):
    ns = types.SimpleNamespace(**dict(zip(names, refs)), **settings)
    fits = ns.fits
    ns.strip = ns.images.shape[0] // ns.micro
    ns.blocks = ns.strip // 32
    ns.width = ns.images.shape[1]
    ns.w = [[getattr(ns, f"w{k}_{i}") for i in range(PIECES[k])] for k in range(4)]
    ns.g = [[getattr(ns, f"g{k}_{i}") for i in range(GRAD_PIECES[k])] for k in range(4)]
    ns.mid = ns.w[0][0].shape[0]
    b, z = place()
    parts = range(ns.micro)
    fields = (ns.ext1, ns.ext2, ns.ext2, ns.ext1)
    loads = [
        pltpu.make_async_copy(source, target, ns.local_sem.at[k])
        for k, (source, target) in enumerate(((ns.images_in, ns.images), (ns.cotangent_in, ns.cotangent)))]
    for load in loads:
        load.start()
    greet(fits)
    halo1, halo2, halo3, halo4 = halos = [
        Halo(field, ns.halo_send.at[k], ns.halo_recv.at[k], ns.blocks) for k, field in enumerate(fields)]
    groups = [Transfer(ns.se_send.at[k], ns.se_recv.at[k]) for k in range(7)]
    ns.third, ns.along, ns.hidden, ns.hidden_back, ns.gate, ns.back, ns.pooled_back = groups
    jobs, wanted = [], {}
    planes = []
    if fits:
        ns.squeeze_halves, ns.excite_halves = [], []
        for k, name, halves in ((4, "squeeze", ns.squeeze_halves), (5, "excite", ns.excite_halves)):
            shard = getattr(ns, f"shard{k}")
            for side, bit in ((0, 4), (1, 2)):
                whole = getattr(ns, f"{name}_half{side}")
                span = whole.shape[2]
                whole[b] = shard[:, side * span:(side + 1) * span]
                halves.append(whole)
                i = len(planes)
                planes.append(PlaneGather(whole, ns.plane_send.at[i], ns.plane_recv.at[i], bit))
                planes[i].own_block()
        ns.gains = [column(ns.vecs[8 + k:9 + k, :], ns.shares[k]) for k in range(4)]
        ns.bias_slots[z] = ns.vecs[0:8, :]
        jobs.append(Gather(ns.bias_slots, ns.bias_rows, ns.gather_send.at[0], ns.gather_recv.at[0]))
        jobs[0].along_row()
        for k in range(4):
            value = standard(getattr(ns, f"shard{k}"), ns.gains[k]).astype(BF)
            wanted[k] = []
            for piece, whole in enumerate(ns.w[k]):
                i, span = len(jobs), whole.shape[1]
                slots = getattr(ns, f"slots{k}_{piece}")
                slots[z] = value[:, piece * span:(piece + 1) * span]
                wanted[k].append(i)
                jobs.append(Gather(slots, whole, ns.gather_send.at[i], ns.gather_recv.at[i]))
                jobs[i].along_row()
        factors = PlaneGather(ns.factor_rows, ns.plane_send.at[4], ns.plane_recv.at[4], 4)
        late = PlaneGather(ns.late_rows, ns.plane_send.at[5], ns.plane_recv.at[5], 2)

    def own(k):
        if fits:
            jobs[k].own_block()

    def onward(k):
        if fits:
            jobs[k].onward()

    def corner(k):
        if fits:
            jobs[k].corner()

    def weight(k):
        for i in wanted.get(k, ()):
            jobs[i].ready()

    ns.bias_sums[...] = jnp.zeros_like(ns.bias_sums)
    ns.widen_sum[...] = jnp.zeros_like(ns.widen_sum)
    ns.second_sum[...] = jnp.zeros_like(ns.second_sum)
    halo1.clear_ends()
    halo2.clear_ends()
    loads[0].wait()
    own(0)

    def first_act(i, carry):
        rows = tile(i, 32)
        ns.act0[rows, :] = (act_only(ns.images[rows, :].astype(F32)) * beta_in).astype(BF)
        return carry

    lax.fori_loop(0, ns.images.shape[0] // 32, first_act, 0)
    for job in planes:
        job.onward()
    own(1)
    onward(0)
    own(2)
    onward(1)
    corner(0)
    own(3)
    for job in planes:
        job.corner()
    onward(2)
    onward(3)
    own(4)
    for job in planes:
        job.ready()
    prepare_maps(ns)
    corner(1)
    corner(2)
    corner(3)
    if fits:
        jobs[0].ready()
        for k in range(6):
            share, row = ns.shares[k], None if k < 4 else z
            width = share * (ns.devices if k < 4 else ns.devices // 4)
            shares = ns.bias_rows[pl.ds(k, ns.devices, stride=8), :]
            ns.brow[k:k + 1, 0:width] = from_shares(shares, share, width, row)
        ns.skip = ns.vecs[6:7, 0:1]
    else:
        ns.skip = ns.brow[6:7, 0:1]
    weight(0)
    narrow_part(ns, 0)
    halo1.start(0)
    own(5)
    narrow_part(ns, 1)
    halo1.start(1)
    onward(4)
    own(6)
    onward(5)
    corner(4)
    weight(1)

    def first_part(part):
        halo1.arrived(part)
        build_columns(ns.ext1, ns.first_cols, ns.bucket, part, ns.blocks, False)
        group_part(ns, part, 1, ns.first_cols, ns.ext2, ns.slope1)
        halo2.start(part)

    def second_part(part):
        halo2.arrived(part)
        build_columns(ns.ext2, ns.cols, ns.bucket, part, ns.blocks, False)
        group_part(ns, part, 2, ns.cols, ns.act3, ns.slope2)

    first_part(0)
    first_part(1)
    onward(6)
    corner(5)
    weight(2)
    second_part(0)
    corner(6)
    second_part(1)
    send_third(ns)
    loads[1].wait()
    weight(3)
    scatters = []
    if fits:
        for k, piece in SCATTERS:
            name = len(scatters)
            refs_of = [getattr(ns, f"{kind}{name}") for kind in ("mate", "diagonal", "sides", "pieces", "landed")]
            whole = ns.bias_parts if k is None else ns.g[k][piece]
            scatters.append(Scatter(whole, *refs_of, ns.scatter_send.at[name], ns.scatter_recv.at[name]))

    def to_mate(k):
        if fits:
            scatters[k].to_mate()

    def diagonals(k):
        if fits:
            scatters[k].diagonals()

    def sides(k):
        if fits:
            scatters[k].to_sides()

    def along_row(k):
        if fits:
            scatters[k].along_row()

    for halo in (halo1, halo2):
        for part in parts:
            halo.close(part)
    widen_part(ns, 0)
    squeeze_images(ns)
    widen_part(ns, 1)
    send_along(ns)
    excite_images(ns)
    take_gates(ns)
    excite_back(ns)
    if fits:
        factors.own_block()
    for part in parts:
        branch_back(ns, part)
    widen_grad(ns)
    to_mate(0)
    squeeze_back(ns)
    if fits:
        factors.onward()
    for part in parts:
        widen_back(ns, part)
    diagonals(0)
    ns.back.arrived(0, 1, 2)
    ns.third_pooled[...] = total_of(ns.back_slots)
    stores = []

    def store(source, target, start, size):
        rows = pl.ds(start, size)
        stores.append(pltpu.make_async_copy(source.at[rows], target.at[rows], ns.local_sem.at[len(stores)]))
        stores[-1].start()

    def third_grad(part):
        third_back(ns, part)
        halo3.start(part)

    def second_grad():
        group_grad(ns, ns.ext2, ns.cols, 2)
        to_mate(1)

    def second_back(part):
        halo3.arrived(part)
        build_columns(ns.ext2, ns.cols, ns.bucket, part, ns.blocks, True)
        group_back(ns, part, 2, ns.slope1, ns.ext1)
        halo4.start(part)

    def first_grad():
        group_grad(ns, ns.ext1, ns.first_cols, 1)
        to_mate(2)

    def first_back(part):
        halo4.arrived(part)
        build_columns(ns.ext1, ns.cols, ns.bucket, part, ns.blocks, True)
        group_back(ns, part, 1, ns.slope0, ns.act3)

    def narrow_piece(i):
        narrow_grad(ns, i)
        to_mate(3 + i)

    def bias_parts():
        ns.bias_sums[2:3, 0:ns.mid] = jnp.sum(ns.second_sum[...], axis=0, keepdims=True)
        ns.bias_sums[3:4, :] = jnp.sum(ns.widen_sum[...], axis=0, keepdims=True) + ns.pooled_sum[...]
        if fits:
            for k in range(6):
                share, row = ns.shares[k], None if k < 4 else z
                vector = ns.bias_sums[k:k + 1, 0:share * (ns.devices if k < 4 else ns.devices // 4)]
                ns.bias_parts[pl.ds(k, ns.devices, stride=8), :] = to_shares(vector, ns.devices, share, row)
            ns.bias_parts[pl.ds(6, ns.devices, stride=8), :] = jnp.broadcast_to(
                ns.bias_sums[6:7, 0:128], (ns.devices, 128))
            ns.bias_parts[pl.ds(7, ns.devices, stride=8), :] = jnp.zeros((ns.devices, 128), F32)
            to_mate(6)

    def input_grad(part):
        input_back(ns, part)
        store(ns.dx, ns.dx_to, part * ns.strip, ns.strip)

    def output():
        add_branch(ns)
        store(ns.out, ns.out_to, 0, 2 * ns.strip)

    def settle(k, total):
        kernel_grad, gain_grad = standard_back(getattr(ns, f"shard{k}"), ns.gains[k], total)
        ns.grad_out[k][...] = kernel_grad
        ns.small_out[8 + k:9 + k, :] = as_row(gain_grad, ns.shares[k])

    def settle_widen():
        factors.ready()
        late.ready()
        settle(3, scatters[0].total() + excite_grads(ns))

    def settle_narrow():
        settle(0, jnp.concatenate([scatters[3 + i].total() for i in range(GRAD_PIECES[0])], axis=1))

    def settle_biases():
        ns.small_out[0:8, :] = scatters[6].total()

    third_grad(0)
    third_grad(1)
    take_pooled(ns)
    if fits:
        late.own_block()
        factors.corner()
    second_grad()
    sides(0)
    output()
    diagonals(1)
    second_back(0)
    if fits:
        late.onward()
    second_back(1)
    sides(1)
    first_grad()
    first_back(0)
    diagonals(2)
    first_back(1)
    along_row(0)
    narrow_piece(0)
    narrow_piece(1)
    sides(2)
    narrow_piece(2)
    diagonals(3)
    diagonals(4)
    diagonals(5)
    bias_parts()
    sides(3)
    input_grad(0)
    sides(4)
    diagonals(6)
    sides(5)
    along_row(1)
    input_grad(1)
    along_row(3)
    sides(6)
    along_row(4)
    along_row(2)
    if fits:
        late.corner()
    along_row(5)
    along_row(6)
    if fits:
        settle(2, scatters[1].total())
    if fits:
        settle(1, scatters[2].total())
    if fits:
        settle_widen()
    if fits:
        settle_biases()
    if fits:
        settle_narrow()
    if fits:
        for job in scatters + jobs + planes + [factors, late]:
            job.close()
    else:
        ns.factor_out[:, :ns.factor_at[-1]] = ns.factor_rows[b]
        ns.factor_out[:, ns.factor_at[-1]:] = ns.late_rows[b]
        ns.bias_sums_out[...] = ns.bias_sums[...]
    for halo in (halo3, halo4):
        for part in parts:
            halo.close(part)
    for group in groups:
        group.close()
    for made in stores:
        made.wait()


PIECES = (3, 1, 1, 1)
GRAD_PIECES = (3, 1, 1, 1)
SCATTERS = ((3, 0), (2, 0), (1, 0), (0, 0), (0, 1), (0, 2), (None, 0))


def hand_over(*refs):
    small, wholes, rest = refs[8], refs[:8], refs[9:]
    for source, target in zip(wholes[:2], rest[:2]):
        target[...] = source[...]

    @pl.when(pl.program_id(0) == 0)
    def _():
        for source, target in zip(wholes[2:], rest[2:8]):
            target[...] = source[...]
        for k, target in enumerate(rest[8:12]):
            target[...] = small[8 + k:9 + k, 0:target.shape[1]]
        for k, target in enumerate(rest[12:18]):
            target[...] = small[k:k + 1, 0:target.shape[1]]
        rest[18][...] = small[6:7, 0:1]


def own_results(got, shares):
    steps = 4
    large = pl.BlockSpec((got[0].shape[0] // steps, got[0].shape[1]), lambda i: (i, 0))
    row = [jax.ShapeDtypeStruct((1, share), F32) for share in shares]
    like = [jax.ShapeDtypeStruct(value.shape, value.dtype) for value in got[:8]]
    results = like + row[:4] + row + [jax.ShapeDtypeStruct((1, 1), F32)]

    def specs(values):
        return [large] * 2 + [pl.BlockSpec(value.shape, lambda i: (0, 0)) for value in values[2:]]

    return pl.pallas_call(
        hand_over, grid=(steps,), out_shape=results, in_specs=specs(got), out_specs=specs(results))(*got)


def run_block(images, bucket, cotangent, kernels, vectors, devices, fits):
    micro, blocks, strip, width = images.shape
    total = micro * blocks * strip
    mid = kernels[0].shape[0] * (devices if fits else 1)
    quarter = devices // 4
    shares = [k.shape[0] // (1 if fits else devices if i < 4 else quarter) for i, k in enumerate(kernels)]
    vmem = pl.BlockSpec(memory_space=pltpu.VMEM)
    smem = pl.BlockSpec(memory_space=pltpu.SMEM)
    anywhere = pl.BlockSpec(memory_space=pl.ANY)
    spans = [quarter * shares[5], mid, width, mid]
    factor_at = [sum(spans[:k]) for k in range(5)]
    late_width = quarter * (shares[5] + shares[4])
    names, specs, args = [], [], []

    def operand(name, value, spec=vmem):
        names.append(name)
        specs.append(spec)
        args.append(value)

    operand("bucket", bucket, smem)
    operand("images_in", images.reshape(total, width), anywhere)
    operand("cotangent_in", cotangent.reshape(total, width), anywhere)
    for k, kernel in enumerate(kernels):
        if fits:
            operand(f"shard{k}", kernel)
        elif k < 4:
            for i, piece in enumerate(jnp.split(kernel, PIECES[k], axis=1)):
                operand(f"w{k}_{i}", piece)
        else:
            operand(("squeeze", "excite_whole")[k - 4], kernel)
    operand("vecs" if fits else "brow", vectors)
    outs = []

    def result(name, shape, dtype):
        names.append(name)
        outs.append(jax.ShapeDtypeStruct(shape, dtype))

    result("out_to", (total, width), BF)
    result("dx_to", (total, width), BF)
    if fits:
        for k in range(6):
            result(f"grad_out{k}", kernels[k].shape, F32)
        result("small_out", (16, 128), F32)
    else:
        for k in range(4):
            for i in range(GRAD_PIECES[k]):
                result(f"g{k}_{i}", (kernels[k].shape[0], kernels[k].shape[1] // GRAD_PIECES[k]), BF)
        result("factor_out", (micro * blocks, factor_at[-1] + late_width), BF)
        result("bias_sums_out", (8, width), F32)
    scratch = []

    def keep(name, shape, dtype):
        names.append(name)
        scratch.append(pltpu.VMEM(shape, dtype))

    images_here = micro * blocks
    whole_shapes = [(s * devices, k.shape[1]) for s, k in zip(shares, kernels)]
    if fits:
        for k, shape in enumerate(whole_shapes[:4]):
            for i in range(PIECES[k]):
                keep(f"w{k}_{i}", (shape[0], shape[1] // PIECES[k]), BF)
                keep(f"slots{k}_{i}", (4, shares[k], shape[1] // PIECES[k]), BF)
        keep("bias_slots", (4, 8, 128), F32)
        keep("bias_rows", (devices * 8, 128), F32)
        keep("brow", (8, width), F32)
        for k in range(4):
            for i in range(GRAD_PIECES[k]):
                keep(f"g{k}_{i}", (whole_shapes[k][0], whole_shapes[k][1] // GRAD_PIECES[k]), BF)
        keep("squeeze", (quarter * shares[4], width), BF)
        for side in (0, 1):
            keep(f"squeeze_half{side}", (quarter, shares[4], width // 2), BF)
            keep(f"excite_half{side}", (quarter, shares[5], mid // 2), BF)
        keep("bias_parts", (devices * 8, 128), F32)
        for i, (k, piece) in enumerate(SCATTERS):
            share, span, dtype = (8, 128, F32) if k is None else (shares[k], whole_shapes[k][1] // GRAD_PIECES[k], BF)
            keep(f"mate{i}", (4, 4 * share, span), dtype)
            keep(f"diagonal{i}", (2, 2 * share, span), dtype)
            keep(f"sides{i}", (2, 4 * share, span), dtype)
            keep(f"pieces{i}", (4, share, span), dtype)
            keep(f"landed{i}", (3, share, span), dtype)
    for name in ("images", "cotangent", "out", "dx"):
        keep(name, (total, width), BF)
    keep("act0", (total, width), BF)
    for name in ("slope0", "slope1", "slope2", "act3"):
        keep(name, (total, mid), BF)
    for name in ("ext1", "ext2"):
        keep(name, (images_here, 64, mid), BF)
    for name in ("first_cols", "cols"):
        keep(name, (mid // GW, total, TAPS * GW), BF)
    keep("third_sums", (images_here, mid), F32)
    keep("third_pooled", (images_here, mid), F32)
    keep("third_slots", (4, images_here, mid), BF)
    keep("along_sums", (images_here, width), F32)
    keep("gates", (images_here, width), F32)
    keep("sigmoid", (images_here, quarter * shares[5]), F32)
    keep("squeeze_slope", (images_here, quarter * shares[4]), F32)
    keep("widen_sum", (8, width), F32)
    keep("second_sum", (8, mid), F32)
    keep("pooled_sum", (1, width), F32)
    keep("bias_sums", (8, width), F32)
    keep("order", (mid, mid), BF)
    keep("excite", (quarter * shares[5], mid), BF)
    keep("pooled_out", (4, images_here, quarter * shares[5]), BF)
    keep("pooled_in", (3, images_here, quarter * shares[5]), BF)
    keep("along_out", (4, images_here, quarter * shares[5]), BF)
    keep("along_in", (3, images_here, quarter * shares[5]), BF)
    keep("hidden_slots", (4, images_here, quarter * shares[4]), BF)
    keep("hidden_out", (4, images_here, quarter * shares[4]), BF)
    keep("hidden_in", (3, images_here, quarter * shares[4]), BF)
    keep("gate_slots", (4, images_here, quarter * shares[5]), BF)
    keep("back_slots", (4, images_here, mid), BF)
    keep("factor_rows", (quarter, images_here, factor_at[-1]), BF)
    keep("late_rows", (quarter, images_here, late_width), BF)
    for name, shape in (
        ("gather_send", (9, 11)), ("gather_recv", (9, 11)), ("scatter_send", (7, 13)), ("scatter_recv", (7, 13)),
        ("local_sem", (4,)),
        ("plane_send", (6, 7)), ("plane_recv", (6, 7)),
        ("halo_send", (4, micro, 2)), ("halo_recv", (4, micro, 2)), ("se_send", (7, 3)), ("se_recv", (7, 3)),
    ):
        names.append(name)
        scratch.append(pltpu.SemaphoreType.DMA(shape))
    settings = dict(fits=fits, devices=devices, micro=micro, shares=shares, factor_at=factor_at)

    def kernel(*refs):
        by_name = dict(zip(names, refs))
        extra = {}
        if fits:
            extra["grad_out"] = [by_name[f"grad_out{k}"] for k in range(6)]
        block_kernel(list(by_name) + list(extra), settings, *by_name.values(), *extra.values())

    return pl.pallas_call(
        kernel,
        out_shape=outs,
        in_specs=specs,
        out_specs=[anywhere] * 2 + [vmem] * (len(outs) - 2),
        scratch_shapes=scratch,
        compiler_params=pltpu.CompilerParams(
            collective_id=0, has_side_effects=True, vmem_limit_bytes=63 << 20),
    )(*args)


def scaled_std(kernel, gain):
    fan = kernel.shape[1]
    center = kernel - jnp.mean(kernel, axis=1, keepdims=True)
    spread = jnp.mean(jnp.square(center), axis=1, keepdims=True)
    return gain[:, None] * center * lax.rsqrt(fan * spread + eps_std)


def body(
    images, bucket, cotangent,
    narrow_kernel, narrow_gain, narrow_bias, first_kernel, first_gain, first_bias,
    second_kernel, second_gain, second_bias, widen_kernel, widen_gain, widen_bias,
    squeeze_kernel, squeeze_bias, excite_kernel, excite_bias, skip_gain,
):
    axes = ("batch", "row")
    devices = lax.axis_size(axes)
    fits = lax.axis_size("batch") == 8
    shape = images.shape
    kernels = [narrow_kernel, first_kernel, second_kernel, widen_kernel]
    maps = [squeeze_kernel, excite_kernel]
    gains = [narrow_gain, first_gain, second_gain, widen_gain]
    biases = [narrow_bias, first_bias, second_bias, widen_bias, squeeze_bias, excite_bias]
    if fits:
        rows = dict(enumerate(biases + [skip_gain])) | {8 + k: gain for k, gain in enumerate(gains)}
        vectors = sum(
            lax.pad(row.astype(F32)[None], jnp.zeros((), F32), ((k, 15 - k, 0), (0, 128 - row.shape[0], 0)))
            for k, row in rows.items())
        got = run_block(images, bucket, cotangent, kernels + maps, vectors, devices, True)
        got = own_results(got, [k.shape[0] for k in kernels + maps])
        output, input_grad = got[0], got[1]
        kernel_grads, gain_grads = got[2:8], [g.reshape(-1) for g in got[8:12]]
        bias_grads, skip_grad = [g.reshape(-1) for g in got[12:18]], got[18].reshape(1)
    else:
        gather = functools.partial(lax.all_gather, axis_name=axes, axis=0, tiled=True)
        scatter = functools.partial(lax.psum_scatter, axis_name=axes, scatter_dimension=0, tiled=True)
        floats = [(k.astype(F32), g.astype(F32)) for k, g in zip(kernels, gains)]
        of_row = functools.partial(lax.all_gather, axis_name="batch", axis=0, tiled=True)
        wholes = [gather(scaled_std(k, g).astype(BF)) for k, g in floats] + [of_row(m) for m in maps]
        width = shape[3]
        rows = [gather(bias).astype(F32) for bias in biases[:4]] + [of_row(bias).astype(F32) for bias in biases[4:]]
        rows += [skip_gain.astype(F32), jnp.zeros((1,), F32)]
        vectors = jnp.stack([jnp.pad(row, (0, width - row.shape[0])) for row in rows])
        got = run_block(images, bucket, cotangent, wholes, vectors, devices, False)
        output, input_grad = got[0], got[1]
        got = list(got)
        got[2:2 + GRAD_PIECES[0]] = [jnp.concatenate(got[2:2 + GRAD_PIECES[0]], axis=1)]
        totals = [scatter(g.astype(F32)) for g in got[2:6]]
        sums = got[7]
        to_row_owner = functools.partial(lax.psum_scatter, axis_name="batch", scatter_dimension=0, tiled=True)
        bias_grads = [(scatter if k < 4 else to_row_owner)(sums[k, :wholes[k].shape[0]]) for k in range(6)]
        skip_grad = lax.psum(sums[6, 0:1], axes)
        span, mid = maps[1].shape[0] * devices // 4, wholes[0].shape[0]
        values = of_row(got[6])
        cuts = [span, span + mid, span + mid + width, span + 2 * mid + width, 2 * span + 2 * mid + width]
        excited, hidden, pooled, third, pooled_grad, squeezed = jnp.split(values, cuts, axis=1)

        def own_rows(own, other, share):
            mine = lax.dynamic_slice_in_dim(own, lax.axis_index("batch") * share, share, axis=1)
            return dot(mine, other, TN)

        totals[3] += own_rows(pooled_grad, third, widen_kernel.shape[0])
        pulled = [jax.vjp(scaled_std, k, g)[1](t) for (k, g), t in zip(floats, totals)]
        kernel_grads, gain_grads = [p[0] for p in pulled], [p[1] for p in pulled]
        kernel_grads.append(own_rows(squeezed, pooled, squeeze_kernel.shape[0]))
        kernel_grads.append(own_rows(excited, hidden, excite_kernel.shape[0]))
    return (
        output.reshape(shape), input_grad.reshape(shape),
        kernel_grads[0], gain_grads[0], bias_grads[0],
        kernel_grads[1], gain_grads[1], bias_grads[1],
        kernel_grads[2], gain_grads[2], bias_grads[2],
        kernel_grads[3], gain_grads[3], bias_grads[3],
        kernel_grads[4], bias_grads[4], kernel_grads[5], bias_grads[5],
        skip_grad,
    )


def solution(mesh):
    maps, shared = P(None, "batch", "row", None), P(("batch", "row"))
    rows = P(("batch", "row"), None)
    weight = (rows, shared, shared)
    return jax.shard_map(
        body,
        mesh=mesh,
        in_specs=(maps, P(None, "batch"), maps, *weight * 4, rows, shared, rows, shared, P()),
        out_specs=(maps, maps, *weight * 4, rows, shared, rows, shared, P()),
        check_vma=False,
    )
```
